512 devices in a mesh: feat: 16 (over x_hi, z), tok: 32 (over x_lo, y, core).
Axes of the slice: x: 4 (x_hi: 2, x_lo: 2; x = x_hi * 2 + x_lo), y: 8, z: 8, core: 2. Of those that a mesh axis runs over, the one named last changes fastest.
Arguments:
- activations: bfloat16 [4096, 16384], P('tok', 'feat'), may hold values from -8 to 8
- act_basis: bfloat16 [32, 512, 512], P('feat'), may hold values from -0.25 to 0.25
- gradients: bfloat16 [4096, 8192], P('tok', 'feat'), may hold values from -8 to 8
- grad_basis: bfloat16 [8192, 512], P('feat'), may hold values from -0.25 to 0.25
Outputs:
- moments: float32 [16384, 8192], P('feat', 'tok')
The draws below stay inside these ranges and needn't reach their ends.
All inputs are finite; a program needn't handle non-finite values.
Results may differ from the reference program's by a relative error of at most 0.0003.
Values may be sent and summed in bfloat16 or wider, within the bound.
No kernel may reach another device: no remote copies, remote signals or barrier semaphores. Data moves between devices by JAX's collectives and lax.ppermute only.
A program may use at most 64 MiB of HBM per device.

```python
import math
import jax
import jax.numpy as jnp

BLOCK = 512
DA = 16384
DG = 8192
TOKENS = 4096


def draw_activations(key, part):
    key = jax.random.fold_in(key, 11)
    keys = jax.random.split(key, 3)
    base = jax.random.normal(keys[0], (TOKENS, DA), jnp.float32)
    row = jnp.exp(jax.random.uniform(keys[1], (TOKENS, 1), jnp.float32, math.log(0.8), math.log(1.25)))
    column = jnp.exp(jax.random.uniform(keys[2], (1, DA), jnp.float32, math.log(0.6), math.log(1.6)))
    return jnp.clip(base * row * column, -8.0, 8.0).astype(jnp.bfloat16)


def draw_gradients(key, part):
    key = jax.random.fold_in(key, 23)
    keys = jax.random.split(key, 3)
    base = jax.random.normal(keys[0], (TOKENS, DG), jnp.float32)
    row = jnp.exp(jax.random.uniform(keys[1], (TOKENS, 1), jnp.float32, math.log(0.8), math.log(1.25)))
    column = jnp.exp(jax.random.uniform(keys[2], (1, DG), jnp.float32, math.log(0.6), math.log(1.6)))
    return jnp.clip(base * row * column, -8.0, 8.0).astype(jnp.bfloat16)


def shard_levels(stream_key, shape, cuts, low, largest):
    def one(position, blocks):
        heights = jax.random.uniform(jax.random.fold_in(jax.random.fold_in(stream_key, 6), position), (blocks,), jnp.float32, low / len(cuts), largest / len(cuts))
        return jnp.repeat(jnp.exp(heights), shape[position] // blocks).reshape((-1,) + (1,) * (len(shape) - position - 1))

    gain = one(*cuts[0])
    for cut in cuts[1:]:
        gain = gain * one(*cut)
    return gain


def bell_draw(own_key, shape, spread, most, pieces=(), kind=jnp.bfloat16):
    entries = jax.random.normal(own_key, shape, jnp.float32) * spread
    if len(pieces) > 0:
        entries = shard_levels(own_key, shape, pieces, -0.22, 0.18) * entries
    return jnp.clip(entries, min=-most, max=most).astype(kind)


def setup_inputs(seed: int = 0) -> dict:
    splits = jax.random.split(jax.random.key(seed), 5)
    return {
        "activations": draw_activations(jax.random.fold_in(splits[4], 71), 0),
        "act_basis": bell_draw(splits[1], (DA // BLOCK, BLOCK, BLOCK), BLOCK ** -0.5, 0.25, ((0, 16),)),
        "gradients": draw_gradients(jax.random.fold_in(splits[4], 71), 0),
        "grad_basis": bell_draw(splits[3], (DG, BLOCK), BLOCK ** -0.5, 0.25, ((0, 16),)),
    }


def reference(activations, act_basis, gradients, grad_basis):
    act_blocks = activations.astype(jnp.float32).reshape(TOKENS, DA // BLOCK, BLOCK)
    act_rot = jnp.einsum("tbk,bkj->tbj", act_blocks, act_basis.astype(jnp.float32)).reshape(TOKENS, DA)
    act_sq = (act_rot * act_rot).astype(jnp.bfloat16)
    grad_blocks = gradients.astype(jnp.float32).reshape(TOKENS, DG // BLOCK, BLOCK)
    grad_mats = grad_basis.astype(jnp.float32).reshape(DG // BLOCK, BLOCK, BLOCK)
    grad_rot = jnp.einsum("tbk,bkj->tbj", grad_blocks, grad_mats).reshape(TOKENS, DG)
    grad_sq = (grad_rot * grad_rot).astype(jnp.bfloat16)
    moments = jnp.dot(act_sq.T, grad_sq, preferred_element_type=jnp.float32)
    return moments / TOKENS
```

```python
import functools

import jax
import jax.numpy as jnp
import numpy as np
from jax import lax
from jax.experimental import pallas as pl
from jax.experimental.pallas import tpu as pltpu
from jax.sharding import Mesh
from jax.sharding import PartitionSpec as P

BLOCK = 512
TOKENS = 4096
XH, Z, XL, Y, C = 2, 8, 2, 8, 2


def shift(x, axis, size, step):
    return lax.ppermute(x, axis, [(i, (i + step) % size) for i in range(size)])


def transpose_chips(x):
    perm = []
    for xh in range(XH):
        for z in range(Z):
            for xl in range(XL):
                for y in range(Y):
                    src = ((xh * Z + z) * XL + xl) * Y + y
                    dst = ((xl * Z + y) * XL + xh) * Y + z
                    perm.append((src, dst))
    return lax.ppermute(x, ("xh", "z", "xl", "y"), perm)


def product_kernel(idx_ref, act_ref, g0_ref, g1_ref, out_ref):
    step = pl.program_id(0)
    act = jnp.concatenate([act_ref[0, 0], act_ref[0, 1]], axis=1)
    grad = jnp.concatenate([g0_ref[0], g1_ref[0]], axis=0)
    part = jnp.dot(act, grad, preferred_element_type=jnp.float32)

    @pl.when(step == 0)
    def _():
        out_ref[...] = part

    @pl.when(step != 0)
    def _():
        out_ref[...] += part


def product(idx, act_all, grad_all):
    _, _, width, rows = act_all.shape
    cols = grad_all.shape[2] // 2
    grid_spec = pltpu.PrefetchScalarGridSpec(
        num_scalar_prefetch=1,
        grid=(Y,),
        in_specs=[
            pl.BlockSpec((1, 2, width, rows), lambda k, idx: (k, 0, 0, 0)),
            pl.BlockSpec((1, rows, cols), lambda k, idx: (idx[2 * k], 0, idx[2 * Y])),
            pl.BlockSpec((1, rows, cols), lambda k, idx: (idx[2 * k + 1], 0, idx[2 * Y])),
        ],
        out_specs=pl.BlockSpec((width, cols), lambda k, idx: (0, 0)),
    )
    return pl.pallas_call(
        product_kernel,
        grid_spec=grid_spec,
        out_shape=jax.ShapeDtypeStruct((width, cols), jnp.float32),
        compiler_params=pltpu.CompilerParams(
            dimension_semantics=("arbitrary",), vmem_limit_bytes=32 * 1024 * 1024
        ),
        cost_estimate=pl.CostEstimate(
            flops=2 * width * cols * rows * 2 * Y,
            bytes_accessed=act_all.size * 2 + grad_all.size + width * cols * 4,
            transcendentals=0,
        ),
    )(idx, act_all, grad_all, grad_all)


def per_device(activations, act_basis, gradients, grad_basis):
    rows, act_width = activations.shape
    act_blocks = activations.reshape(rows, act_width // BLOCK, BLOCK)
    act_rot = jnp.einsum("tbk,bkj->bjt", act_blocks, act_basis, preferred_element_type=jnp.float32)
    act_sq = (act_rot * act_rot).astype(jnp.bfloat16).reshape(act_width, rows)
    act_pair = jnp.stack([act_sq, shift(act_sq, "xl", XL, 1)])
    act_all = lax.all_gather(act_pair, "y", axis=0)

    grad_rot = jnp.dot(gradients, grad_basis, preferred_element_type=jnp.float32)
    grad_sq = (grad_rot * grad_rot).astype(jnp.bfloat16)
    own = transpose_chips(grad_sq)
    near = {0: own}
    for d in (1, 7, 4, 2, 6, 3, 5):
        near[d] = shift(own, "z", Z, d)
    far = {}
    for group in ((0,), (1, 7, 4), (2, 6, 3, 5)):
        sent = near[group[0]][None] if len(group) == 1 else jnp.stack([near[d] for d in group])
        got = shift(sent, "xh", XH, 1)
        for i, d in enumerate(group):
            far[d] = got[i]
    grad_all = jnp.stack([near[d] for d in range(Z)] + [far[d] for d in range(Z)])

    xh, z, xl = lax.axis_index("xh"), lax.axis_index("z"), lax.axis_index("xl")
    c = lax.axis_index("c")
    y_pos = jnp.arange(Y, dtype=jnp.int32)[:, None]
    half = jnp.arange(2, dtype=jnp.int32)[None, :]
    place = (half ^ xl ^ xh) * Z + (z - y_pos) % Z
    place = place.reshape(2 * Y).astype(jnp.int32)
    other = product(jnp.concatenate([place, (1 - c)[None]]), act_all, grad_all)
    got = shift(other, "c", C, 1)
    mine = product(jnp.concatenate([place, c[None]]), act_all, grad_all)
    return (mine + got) / TOKENS


def solution(mesh):
    chips = Mesh(mesh.devices.reshape(XH, Z, XL, Y, C), ("xh", "z", "xl", "y", "c"))
    feat, tok = ("xh", "z"), ("xl", "y", "c")
    return jax.shard_map(
        per_device,
        mesh=chips,
        in_specs=(P(tok, feat), P(feat, None, None), P(tok, feat), P(feat, None)),
        out_specs=P(feat, tok),
        check_vma=False,
    )
```

```python
import jax
import jax.numpy as jnp
from jax import lax
from jax.experimental import pallas as pl
from jax.experimental.pallas import tpu as pltpu
from jax.sharding import Mesh
from jax.sharding import PartitionSpec as P

BLOCK = 512
TOKENS = 4096
XH, Z, XL, Y, C = 2, 8, 2, 8, 2


def shift(x, axis, size, step):
    return lax.ppermute(x, axis, [(i, (i + step) % size) for i in range(size)])


def transpose_chips(x):
    perm = []
    for xh in range(XH):
        for z in range(Z):
            for xl in range(XL):
                for y in range(Y):
                    src = ((xh * Z + z) * XL + xl) * Y + y
                    dst = ((xl * Z + y) * XL + xh) * Y + z
                    perm.append((src, dst))
    return lax.ppermute(x, ("xh", "z", "xl", "y"), perm)


def vmem():
    return pl.BlockSpec(memory_space=pltpu.VMEM)


def products(places, pieces, grad_all, cols, acc=None, add=None, scale=None):
    _, width, rows = pieces[0].shape
    out_cols = grad_all.shape[2] if cols is None else grad_all.shape[2] // 2
    n = len(pieces)
    extra = [] if acc is None else [acc]
    extra += [] if add is None else [add]

    def kernel(*refs):
        places_ref, piece_refs, grad_ref = refs[0], refs[1 : 1 + n], refs[1 + n]
        out_ref = refs[-1]
        if cols is None:
            where = slice(None)
        else:
            where = pl.ds(pl.multiple_of(places_ref[2 * n] * out_cols, out_cols), out_cols)
        grads = []
        for i in range(n):
            grads.append(grad_ref[places_ref[2 * i], :, where])
            grads.append(grad_ref[places_ref[2 * i + 1], :, where])
        grad = jnp.concatenate(grads, axis=0)
        tile = 128

        @pl.loop(0, width // tile)
        def _(t):
            at = pl.ds(pl.multiple_of(t * tile, tile), tile)
            lhs = []
            for ref in piece_refs:
                lhs += [ref[0, at, :], ref[1, at, :]]
            total = jnp.dot(
                jnp.concatenate(lhs, axis=1), grad, preferred_element_type=jnp.float32
            )
            if acc is not None:
                total += refs[2 + n][at, :] if cols is None else refs[2 + n][at, where]
            if add is not None:
                total += refs[3 + n][at, :]
            out_ref[at, :] = total if scale is None else total * scale

    size = lambda a: a.size * a.dtype.itemsize
    return pl.pallas_call(
        kernel,
        in_specs=[pl.BlockSpec(memory_space=pltpu.SMEM)] + [vmem()] * (n + 1 + len(extra)),
        out_specs=vmem(),
        out_shape=jax.ShapeDtypeStruct((width, out_cols), jnp.float32),
        compiler_params=pltpu.CompilerParams(vmem_limit_bytes=40 * 1024 * 1024),
        cost_estimate=pl.CostEstimate(
            flops=2 * width * out_cols * rows * 2 * n,
            bytes_accessed=sum(map(size, pieces)) + size(grad_all) + width * out_cols * 4,
            transcendentals=0,
        ),
    )(places, *pieces, grad_all, *extra)


def per_device(activations, act_basis, gradients, grad_basis):
    xh, z, xl, y, c = (lax.axis_index(a) for a in ("xh", "z", "xl", "y", "c"))
    rows, act_width = activations.shape

    grad_rot = jnp.dot(gradients, grad_basis, preferred_element_type=jnp.float32)
    grad_sq = (grad_rot * grad_rot).astype(jnp.bfloat16)
    own = transpose_chips(grad_sq)

    act_blocks = activations.reshape(rows, act_width // BLOCK, BLOCK)
    act_rot = jnp.einsum("tbk,bkj->bjt", act_blocks, act_basis, preferred_element_type=jnp.float32)
    act_sq = (act_rot * act_rot).astype(jnp.bfloat16).reshape(act_width, rows)
    pair = jnp.stack([act_sq, shift(act_sq, "xl", XL, 1)])
    up = [pair]
    down = [pair]
    for _ in range(3):
        up.append(shift(up[-1], "y", Y, 1))
        down.append(shift(down[-1], "y", Y, -1))
    far_up = shift(up[3][0], "y", Y, 1)
    far_down = shift(down[3][1], "y", Y, -1)
    last = jnp.stack([far_up, far_down])

    near = {0: own}
    for d in (1, 7, 2, 6, 3, 5, 4):
        near[d] = shift(own, "z", Z, d)
    far = {}
    for group in ((0,), (1, 7, 2), (6, 3, 5, 4)):
        sent = near[group[0]][None] if len(group) == 1 else jnp.stack([near[d] for d in group])
        got = shift(sent, "xh", XH, 1)
        for i, d in enumerate(group):
            far[d] = got[i]
    grad_all = jnp.stack([near[d] for d in range(Z)] + [far[d] for d in range(Z)])

    def places(offsets, half=None):
        pos = (y - jnp.array(offsets, jnp.int32))[:, None]
        pair_of = jnp.arange(2, dtype=jnp.int32)[None, :]
        at = ((pair_of ^ xl ^ xh) * Z + (z - pos) % Z).reshape(-1)
        if half is not None:
            at = jnp.concatenate([at, half[None]])
        return at.astype(jnp.int32)

    first = products(places([0, 1, -1, 2, -2]), [pair, up[1], down[1], up[2], down[2]], grad_all, None)
    second = products(places([3, -3]), [up[3], down[3]], grad_all, None, acc=first)
    other = products(places([4], 1 - c), [last], grad_all, True, acc=second)
    got = shift(other, "c", C, 1)
    return products(places([4], c), [last], grad_all, True, acc=second, add=got, scale=1.0 / TOKENS)


def solution(mesh):
    chips = Mesh(mesh.devices.reshape(XH, Z, XL, Y, C), ("xh", "z", "xl", "y", "c"))
    feat, tok = ("xh", "z"), ("xl", "y", "c")
    return jax.shard_map(
        per_device,
        mesh=chips,
        in_specs=(P(tok, feat), P(feat, None, None), P(tok, feat), P(feat, None)),
        out_specs=P(feat, tok),
        check_vma=False,
    )
```

```python
import jax
import jax.numpy as jnp
from jax import lax
from jax.experimental import pallas as pl
from jax.experimental.pallas import tpu as pltpu
from jax.sharding import Mesh
from jax.sharding import PartitionSpec as P

BLOCK = 512
TOKENS = 4096
XH, Z, XL, Y, C = 2, 8, 2, 8, 2


def transpose_chips(x):
    perm = []
    for xh in range(XH):
        for z in range(Z):
            for xl in range(XL):
                for y in range(Y):
                    src = ((xh * Z + z) * XL + xl) * Y + y
                    dst = ((xl * Z + y) * XL + xh) * Y + z
                    perm.append((src, dst))
    return lax.ppermute(x, ("xh", "z", "xl", "y"), perm)


def swap(x, axis):
    return lax.ppermute(x, axis, [(0, 1), (1, 0)])


def product_kernel(where_ref, act_ref, grad_ref, out_ref):
    xl, half = where_ref[0], where_ref[1]
    cols = out_ref.shape[1]
    at = pl.ds(pl.multiple_of(half * cols, cols), cols)
    total = None
    for pair in range(2):
        act = jnp.concatenate([act_ref[y, pair] for y in range(Y)], axis=1)
        grad = grad_ref[pair ^ xl, :, at]
        part = jnp.dot(act, grad, preferred_element_type=jnp.float32)
        total = part if total is None else total + part
    out_ref[...] = total


def product(where, act_all, grad_all):
    _, _, width, rows = act_all.shape
    cols = grad_all.shape[2] // 2
    tile = 128
    grid_spec = pltpu.PrefetchScalarGridSpec(
        num_scalar_prefetch=1,
        grid=(width // tile,),
        in_specs=[
            pl.BlockSpec((Y, 2, tile, rows), lambda i, where: (0, 0, i, 0)),
            pl.BlockSpec(grad_all.shape, lambda i, where: (0, 0, 0)),
        ],
        out_specs=pl.BlockSpec((tile, cols), lambda i, where: (i, 0)),
    )
    return pl.pallas_call(
        product_kernel,
        grid_spec=grid_spec,
        out_shape=jax.ShapeDtypeStruct((width, cols), jnp.float32),
        compiler_params=pltpu.CompilerParams(
            dimension_semantics=("arbitrary",), vmem_limit_bytes=56 * 1024 * 1024
        ),
        cost_estimate=pl.CostEstimate(
            flops=2 * width * cols * rows * 2 * Y,
            bytes_accessed=act_all.size * 2 + grad_all.size * 2 + width * cols * 4,
            transcendentals=0,
        ),
    )(where, act_all, grad_all)


def per_device(activations, act_basis, gradients, grad_basis):
    rows, act_width = activations.shape
    xl, c = lax.axis_index("xl"), lax.axis_index("c")

    grad_rot = jnp.dot(gradients, grad_basis, preferred_element_type=jnp.float32)
    grad_sq = (grad_rot * grad_rot).astype(jnp.bfloat16)
    own = transpose_chips(grad_sq)

    act_blocks = activations.reshape(rows, act_width // BLOCK, BLOCK)
    act_rot = jnp.einsum("tbk,bkj->bjt", act_blocks, act_basis, preferred_element_type=jnp.float32)
    act_sq = (act_rot * act_rot).astype(jnp.bfloat16).reshape(act_width, rows)
    act_pair = jnp.stack([act_sq, swap(act_sq, "xl")])
    act_all = lax.all_gather(act_pair, "y", axis=0)

    copies = jnp.broadcast_to(own, (XH * Z,) + own.shape)
    grad_all = lax.all_to_all(copies, ("xh", "z"), 0, 0, tiled=True)
    grad_all = grad_all.reshape(XH, Z * rows, gradients.shape[1])

    other = product(jnp.stack([xl, 1 - c]), act_all, grad_all)
    got = swap(other, "c")
    mine = product(jnp.stack([xl, c]), act_all, grad_all)
    return (mine + got) / TOKENS


def solution(mesh):
    chips = Mesh(mesh.devices.reshape(XH, Z, XL, Y, C), ("xh", "z", "xl", "y", "c"))
    feat, tok = ("xh", "z"), ("xl", "y", "c")
    return jax.shard_map(
        per_device,
        mesh=chips,
        in_specs=(P(tok, feat), P(feat, None, None), P(tok, feat), P(feat, None)),
        out_specs=P(feat, tok),
        check_vma=False,
    )
```

```python
import jax
import jax.numpy as jnp
from jax import lax
from jax.experimental import pallas as pl
from jax.experimental.pallas import tpu as pltpu
from jax.sharding import Mesh
from jax.sharding import PartitionSpec as P

BLOCK = 512
TOKENS = 4096
XH, Z, XL, Y, C = 2, 8, 2, 8, 2


def shift(x, axis, size, step):
    return lax.ppermute(x, axis, [(i, (i + step) % size) for i in range(size)])


def transpose_chips(x):
    perm = []
    for xh in range(XH):
        for z in range(Z):
            for xl in range(XL):
                for y in range(Y):
                    src = ((xh * Z + z) * XL + xl) * Y + y
                    dst = ((xl * Z + y) * XL + xh) * Y + z
                    perm.append((src, dst))
    return lax.ppermute(x, ("xh", "z", "xl", "y"), perm)


def vmem():
    return pl.BlockSpec(memory_space=pltpu.VMEM)


def products(places, pieces, grad_all, halved=False, acc=None, add=None, scale=None):
    _, width, rows = pieces[0].shape
    cols = grad_all.shape[2] // 2 if halved else grad_all.shape[2]
    n = len(pieces)
    extra = [] if acc is None else [acc]
    extra += [] if add is None else [add]
    tile = width // 2

    def kernel(*refs):
        places_ref, piece_refs, grad_ref, out_ref = refs[0], refs[1 : 1 + n], refs[1 + n], refs[-1]
        where = slice(None)
        if halved:
            where = pl.ds(pl.multiple_of(places_ref[2 * n] * cols, cols), cols)
        grad = jnp.concatenate([grad_ref[places_ref[i], :, where] for i in range(2 * n)], axis=0)
        for t in range(width // tile):
            at = slice(t * tile, (t + 1) * tile)
            lhs = jnp.concatenate([ref[k, at] for ref in piece_refs for k in range(2)], axis=1)
            total = jnp.dot(lhs, grad, preferred_element_type=jnp.float32)
            if acc is not None:
                total += refs[2 + n][at, where]
            if add is not None:
                total += refs[3 + n][at]
            out_ref[at] = total if scale is None else total * scale

    def size(a):
        return a.size * a.dtype.itemsize

    return pl.pallas_call(
        kernel,
        in_specs=[pl.BlockSpec(memory_space=pltpu.SMEM)] + [vmem()] * (n + 1 + len(extra)),
        out_specs=vmem(),
        out_shape=jax.ShapeDtypeStruct((width, cols), jnp.float32),
        compiler_params=pltpu.CompilerParams(vmem_limit_bytes=24 * 1024 * 1024),
        cost_estimate=pl.CostEstimate(
            flops=2 * width * cols * rows * 2 * n,
            bytes_accessed=sum(map(size, pieces)) + size(grad_all) + width * cols * 4,
            transcendentals=0,
        ),
    )(places, *pieces, grad_all, *extra)


def per_device(activations, act_basis, gradients, grad_basis):
    xl, y, c = (lax.axis_index(a) for a in ("xl", "y", "c"))
    rows, act_width = activations.shape

    grad_rot = jnp.dot(gradients, grad_basis, preferred_element_type=jnp.float32)
    grad_sq = (grad_rot * grad_rot).astype(jnp.bfloat16)
    activations, grad_sq = lax.optimization_barrier((activations, grad_sq))
    own = transpose_chips(grad_sq)

    act_blocks = activations.reshape(rows, act_width // BLOCK, BLOCK)
    act_rot = jnp.einsum("tbk,bkj->bjt", act_blocks, act_basis, preferred_element_type=jnp.float32)
    act_sq = (act_rot * act_rot).astype(jnp.bfloat16).reshape(act_width, rows)
    pair = jnp.stack([act_sq, shift(act_sq, "xl", XL, 1)])
    up = [pair]
    down = [pair]
    for _ in range(3):
        up.append(shift(up[-1], "y", Y, 1))
        down.append(shift(down[-1], "y", Y, -1))
    last = jnp.stack([shift(up[3][0], "y", Y, 1), shift(down[3][1], "y", Y, -1)])

    own, _ = lax.optimization_barrier((own, pair))
    copies = jnp.broadcast_to(own, (XH * Z,) + own.shape)
    grad_all = lax.all_to_all(copies, ("xh", "z"), 0, 0, tiled=True)
    grad_all = grad_all.reshape(XH * Z, rows, gradients.shape[1])

    def places(offsets, half=None):
        at = [(k ^ xl) * Y + (y + Y - d) % Y for d in offsets for k in range(2)]
        return jnp.stack(at + ([] if half is None else [half])).astype(jnp.int32)

    first = products(places([0, 1, -1, 2, -2]), [pair, up[1], down[1], up[2], down[2]], grad_all)
    second = products(places([3, -3]), [up[3], down[3]], grad_all, acc=first)
    other = products(places([4], 1 - c), [last], grad_all, True, acc=second)
    got = shift(other, "c", C, 1)
    return products(places([4], c), [last], grad_all, True, acc=second, add=got, scale=1.0 / TOKENS)


def solution(mesh):
    chips = Mesh(mesh.devices.reshape(XH, Z, XL, Y, C), ("xh", "z", "xl", "y", "c"))
    feat, tok = ("xh", "z"), ("xl", "y", "c")
    return jax.shard_map(
        per_device,
        mesh=chips,
        in_specs=(P(tok, feat), P(feat, None, None), P(tok, feat), P(feat, None)),
        out_specs=P(feat, tok),
        check_vma=False,
    )
```

```python
import jax
import jax.numpy as jnp
from jax import lax
from jax.experimental import pallas as pl
from jax.experimental.pallas import tpu as pltpu
from jax.sharding import Mesh
from jax.sharding import PartitionSpec as P

BLOCK = 512
TOKENS = 4096
XH, Z, XL, Y, C = 2, 8, 2, 8, 2


def shift(x, axis, size, step):
    return lax.ppermute(x, axis, [(i, (i + step) % size) for i in range(size)])


def transpose_chips(x):
    perm = []
    for xh in range(XH):
        for z in range(Z):
            for xl in range(XL):
                for y in range(Y):
                    src = ((xh * Z + z) * XL + xl) * Y + y
                    dst = ((xl * Z + y) * XL + xh) * Y + z
                    perm.append((src, dst))
    return lax.ppermute(x, ("xh", "z", "xl", "y"), perm)


def products(places, pieces, grad_all):
    width, rows = pieces[0].shape
    cols = grad_all.shape[2] // 2
    n = len(pieces)
    tile = width // 2
    per_group = 4

    def kernel(*refs):
        places_ref, piece_refs = refs[0], refs[1 : 1 + n]
        grad_ref, out_ref, held, grad_held, sems, grad_sem = refs[1 + n :]
        grad_copy = pltpu.make_async_copy(grad_ref, grad_held, grad_sem)
        grad_copy.start()
        copies = [pltpu.make_async_copy(piece_refs[i], held.at[i], sems.at[i]) for i in range(n)]
        for copy in copies:
            copy.start()
        grad_copy.wait()
        where = pl.ds(pl.multiple_of(places_ref[n] * cols, cols), cols)
        for first in range(0, n, per_group):
            group = range(first, min(first + per_group, n))
            grad = jnp.concatenate([grad_held[places_ref[i], :, where] for i in group], axis=0)
            for i in group:
                copies[i].wait()
            for t in range(width // tile):
                at = slice(t * tile, (t + 1) * tile)
                lhs = jnp.concatenate([held[i, at] for i in group], axis=1)
                total = jnp.dot(lhs, grad, preferred_element_type=jnp.float32)
                if first == 0:
                    out_ref[at] = total
                else:
                    out_ref[at] += total

    def size(a):
        return a.size * a.dtype.itemsize

    return pl.pallas_call(
        kernel,
        in_specs=[pl.BlockSpec(memory_space=pltpu.SMEM)]
        + [pl.BlockSpec(memory_space=pltpu.HBM)] * (n + 1),
        out_specs=pl.BlockSpec(memory_space=pltpu.VMEM),
        out_shape=jax.ShapeDtypeStruct((width, cols), jnp.float32),
        scratch_shapes=[
            pltpu.VMEM((n, width, rows), pieces[0].dtype),
            pltpu.VMEM(grad_all.shape, grad_all.dtype),
            pltpu.SemaphoreType.DMA((n,)),
            pltpu.SemaphoreType.DMA,
        ],
        compiler_params=pltpu.CompilerParams(vmem_limit_bytes=24 * 1024 * 1024),
        cost_estimate=pl.CostEstimate(
            flops=2 * width * cols * rows * n,
            bytes_accessed=sum(map(size, pieces)) + size(grad_all) + width * cols * 4,
            transcendentals=0,
        ),
    )(places, *pieces, grad_all)


def per_device(activations, act_basis, gradients, grad_basis):
    xl, y, c = (lax.axis_index(a) for a in ("xl", "y", "c"))
    rows, act_width = activations.shape

    grad_rot = jnp.dot(gradients, grad_basis, preferred_element_type=jnp.float32)
    grad_sq = (grad_rot * grad_rot).astype(jnp.bfloat16)
    own = transpose_chips(grad_sq)

    act_blocks = activations.reshape(rows, act_width // BLOCK, BLOCK)
    act_rot = jnp.einsum("tbk,bkj->bjt", act_blocks, act_basis, preferred_element_type=jnp.float32)
    act_sq = (act_rot * act_rot).astype(jnp.bfloat16).reshape(act_width, rows)
    near_up, near_down = [act_sq], [act_sq]
    for _ in range(3):
        near_up.append(shift(near_up[-1], "y", Y, 1))
        near_down.append(shift(near_down[-1], "y", Y, -1))
    near_up.append(shift(near_up[-1], "y", Y, 1))
    far_up = [shift(act_sq, "xl", XL, 1)]
    far_down = far_up[:]
    for _ in range(3):
        far_up.append(shift(far_up[-1], "y", Y, 1))
        far_down.append(shift(far_down[-1], "y", Y, -1))
    far_down.append(shift(far_down[-1], "y", Y, -1))

    own, _, _, _ = lax.optimization_barrier((own, near_up[1], near_down[1], far_up[0]))
    copies = jnp.broadcast_to(own, (XH * Z,) + own.shape)
    grad_all = lax.all_to_all(copies, ("xh", "z"), 0, 0, tiled=True)
    grad_all = grad_all.reshape(XH * Z, rows, gradients.shape[1])

    pieces, at = [], []
    for k in range(5):
        for way, ring, pair in ((-1, near_up, 0), (1, near_down, 0), (-1, far_up, 1), (1, far_down, 1)):
            if k < len(ring) and (k > 0 or way < 0):
                pieces.append(ring[k])
                at.append((pair ^ xl) * Y + (y + Y + way * k) % Y)

    def places(half):
        return jnp.stack(at + [half]).astype(jnp.int32)

    other = products(places(1 - c), pieces, grad_all)
    got = shift(other, "c", C, 1)
    mine = products(places(c), pieces, grad_all)
    return (mine + got) / TOKENS


def solution(mesh):
    chips = Mesh(mesh.devices.reshape(XH, Z, XL, Y, C), ("xh", "z", "xl", "y", "c"))
    feat, tok = ("xh", "z"), ("xl", "y", "c")
    return jax.shard_map(
        per_device,
        mesh=chips,
        in_specs=(P(tok, feat), P(feat, None, None), P(tok, feat), P(feat, None)),
        out_specs=P(feat, tok),
        check_vma=False,
    )
```

```python
import jax
import jax.numpy as jnp
from jax import lax
from jax.experimental import pallas as pl
from jax.experimental.pallas import tpu as pltpu
from jax.sharding import Mesh
from jax.sharding import PartitionSpec as P

BLOCK = 512
TOKENS = 4096
XH, Z, XL, Y, C = 2, 8, 2, 8, 2


def shift(x, axis, size, step):
    return lax.ppermute(x, axis, [(i, (i + step) % size) for i in range(size)])


def transpose_chips(x):
    chips = XH * Z
    swaps = [[f * chips + m, m * chips + f] for f in range(chips) for m in range(f + 1, chips)]
    fixed = [f * chips + f for f in range(chips)]
    groups = swaps + [[fixed[i], fixed[i + 1]] for i in range(0, chips, 2)]
    f = lax.axis_index("xh") * Z + lax.axis_index("z")
    m = lax.axis_index("xl") * Y + lax.axis_index("y")
    sent = jnp.broadcast_to(x, (2,) + x.shape)
    got = lax.all_to_all(sent, ("xh", "z", "xl", "y"), 0, 0, axis_index_groups=groups)
    return jnp.where(f > m, got[0], jnp.where(f < m, got[1], x))


def products(places, pieces, grad_all):
    width, rows = pieces[0].shape
    cols = grad_all.shape[2] // 2
    n = len(pieces)
    tile = width // 2
    per_group = 4

    def kernel(*refs):
        places_ref, piece_refs = refs[0], refs[1 : 1 + n]
        grad_ref, out_ref, held, grad_held, sems, grad_sem = refs[1 + n :]
        grad_copy = pltpu.make_async_copy(grad_ref, grad_held, grad_sem)
        grad_copy.start()
        copies = [pltpu.make_async_copy(piece_refs[i], held.at[i], sems.at[i]) for i in range(n)]
        for copy in copies:
            copy.start()
        grad_copy.wait()
        where = pl.ds(pl.multiple_of(places_ref[n] * cols, cols), cols)
        for first in range(0, n, per_group):
            group = range(first, min(first + per_group, n))
            grad = jnp.concatenate([grad_held[places_ref[i], :, where] for i in group], axis=0)
            for i in group:
                copies[i].wait()
            for t in range(width // tile):
                at = slice(t * tile, (t + 1) * tile)
                lhs = jnp.concatenate([held[i, at] for i in group], axis=1)
                total = jnp.dot(lhs, grad, preferred_element_type=jnp.float32)
                if first == 0:
                    out_ref[at] = total
                else:
                    out_ref[at] += total

    def size(a):
        return a.size * a.dtype.itemsize

    return pl.pallas_call(
        kernel,
        in_specs=[pl.BlockSpec(memory_space=pltpu.SMEM)]
        + [pl.BlockSpec(memory_space=pltpu.HBM)] * (n + 1),
        out_specs=pl.BlockSpec(memory_space=pltpu.VMEM),
        out_shape=jax.ShapeDtypeStruct((width, cols), jnp.float32),
        scratch_shapes=[
            pltpu.VMEM((n, width, rows), pieces[0].dtype),
            pltpu.VMEM(grad_all.shape, grad_all.dtype),
            pltpu.SemaphoreType.DMA((n,)),
            pltpu.SemaphoreType.DMA,
        ],
        compiler_params=pltpu.CompilerParams(vmem_limit_bytes=56 * 1024 * 1024),
        cost_estimate=pl.CostEstimate(
            flops=2 * width * cols * rows * n,
            bytes_accessed=sum(map(size, pieces)) + size(grad_all) + width * cols * 4,
            transcendentals=0,
        ),
    )(places, *pieces, grad_all)


def per_device(activations, act_basis, gradients, grad_basis):
    xl, y, c = (lax.axis_index(a) for a in ("xl", "y", "c"))
    rows, act_width = activations.shape

    grad_rot = jnp.dot(gradients, grad_basis, preferred_element_type=jnp.float32)
    grad_sq = (grad_rot * grad_rot).astype(jnp.bfloat16)
    own = transpose_chips(grad_sq)

    act_blocks = activations.reshape(rows, act_width // BLOCK, BLOCK)
    act_rot = jnp.einsum("tbk,bkj->bjt", act_blocks, act_basis, preferred_element_type=jnp.float32)
    act_sq = (act_rot * act_rot).astype(jnp.bfloat16).reshape(act_width, rows)
    near_up, near_down = [act_sq], [act_sq]
    for _ in range(3):
        near_up.append(shift(near_up[-1], "y", Y, 1))
        near_down.append(shift(near_down[-1], "y", Y, -1))
    near_up.append(shift(near_up[-1], "y", Y, 1))
    far_up = [shift(act_sq, "xl", XL, 1)]
    far_down = far_up[:]
    for _ in range(3):
        far_up.append(shift(far_up[-1], "y", Y, 1))
        far_down.append(shift(far_down[-1], "y", Y, -1))
    far_down.append(shift(far_down[-1], "y", Y, -1))

    own, _, _, _ = lax.optimization_barrier((own, near_up[1], near_down[1], far_up[0]))
    copies = jnp.broadcast_to(own, (XH * Z,) + own.shape)
    grad_all = lax.all_to_all(copies, ("xh", "z"), 0, 0, tiled=True)
    grad_all = grad_all.reshape(XH * Z, rows, gradients.shape[1])

    pieces, at = [], []
    for k in range(5):
        for way, ring, pair in ((-1, near_up, 0), (1, near_down, 0), (-1, far_up, 1), (1, far_down, 1)):
            if k < len(ring) and (k > 0 or way < 0):
                pieces.append(ring[k])
                at.append((pair ^ xl) * Y + (y + Y + way * k) % Y)

    def places(half):
        return jnp.stack(at + [half]).astype(jnp.int32)

    other = products(places(1 - c), pieces, grad_all)
    got = shift(other, "c", C, 1)
    mine = products(places(c), pieces, grad_all)
    return (mine + got) / TOKENS


def solution(mesh):
    chips = Mesh(mesh.devices.reshape(XH, Z, XL, Y, C), ("xh", "z", "xl", "y", "c"))
    feat, tok = ("xh", "z"), ("xl", "y", "c")
    return jax.shard_map(
        per_device,
        mesh=chips,
        in_specs=(P(tok, feat), P(feat, None, None), P(tok, feat), P(feat, None)),
        out_specs=P(feat, tok),
        check_vma=False,
    )
```

```python
import jax
import jax.numpy as jnp
from jax import lax
from jax.experimental import pallas as pl
from jax.experimental.pallas import tpu as pltpu
from jax.sharding import Mesh
from jax.sharding import PartitionSpec as P

BLOCK = 512
TOKENS = 4096
XH, Z, XL, Y, C = 2, 8, 2, 8, 2


def shift(x, axis, size, step):
    return lax.ppermute(x, axis, [(i, (i + step) % size) for i in range(size)])


def transpose_chips(x):
    chips = XH * Z
    swaps = [[f * chips + m, m * chips + f] for f in range(chips) for m in range(f + 1, chips)]
    fixed = [f * chips + f for f in range(chips)]
    groups = swaps + [[fixed[i], fixed[i + 1]] for i in range(0, chips, 2)]
    f = lax.axis_index("xh") * Z + lax.axis_index("z")
    m = lax.axis_index("xl") * Y + lax.axis_index("y")
    sent = jnp.broadcast_to(x, (2,) + x.shape)
    got = lax.all_to_all(sent, ("xh", "z", "xl", "y"), 0, 0, axis_index_groups=groups)
    return jnp.where(f > m, got[0], jnp.where(f < m, got[1], x))


def products(places, pieces, grad_all, acc=None, vmem_mib=56):
    width, rows = pieces[0].shape
    cols = grad_all.shape[2] // 2
    n = len(pieces)
    tile = width // 2
    per_group = 4

    def kernel(*refs):
        places_ref, piece_refs = refs[0], refs[1 : 1 + n]
        grad_ref = refs[1 + n]
        out_ref, held, grad_held, sems, grad_sems = refs[-5:]
        grad_copies = [
            pltpu.make_async_copy(grad_ref.at[places_ref[i]], grad_held.at[i], grad_sems.at[i]) for i in range(n)
        ]
        copies = [pltpu.make_async_copy(piece_refs[i], held.at[i], sems.at[i]) for i in range(n)]
        if acc is not None:
            half = places_ref[n]
            acc_copy = pltpu.make_async_copy(refs[2 + n].at[half], out_ref, sems.at[n])
            acc_copy.start()
        for i in range(n):
            grad_copies[i].start()
            copies[i].start()
        for first in range(0, n, per_group):
            group = range(first, min(first + per_group, n))
            for i in group:
                grad_copies[i].wait()
                copies[i].wait()
            if acc is None:
                grad = jnp.concatenate([grad_held[i] for i in group], axis=0)
            else:
                where = pl.ds(pl.multiple_of(half * cols, cols), cols)
                grad = jnp.concatenate([grad_held[i, :, where] for i in group], axis=0)
                acc_copy.wait()
            for t in range(width // tile):
                at = slice(t * tile, (t + 1) * tile)
                lhs = jnp.concatenate([held[i, at] for i in group], axis=1)
                total = jnp.dot(lhs, grad, preferred_element_type=jnp.float32)
                if acc is not None:
                    out_ref[at] += total
                elif first == 0:
                    out_ref[0, at] = total[:, :cols]
                    out_ref[1, at] = total[:, cols:]
                else:
                    out_ref[0, at] += total[:, :cols]
                    out_ref[1, at] += total[:, cols:]

    def size(a):
        return a.size * a.dtype.itemsize

    shape = (2, width, cols) if acc is None else (width, cols)
    extra = [] if acc is None else [acc]
    return pl.pallas_call(
        kernel,
        in_specs=[pl.BlockSpec(memory_space=pltpu.SMEM)]
        + [pl.BlockSpec(memory_space=pltpu.HBM)] * (n + 1 + len(extra)),
        out_specs=pl.BlockSpec(memory_space=pltpu.VMEM),
        out_shape=jax.ShapeDtypeStruct(shape, jnp.float32),
        scratch_shapes=[
            pltpu.VMEM((n, width, rows), pieces[0].dtype),
            pltpu.VMEM((n,) + grad_all.shape[1:], grad_all.dtype),
            pltpu.SemaphoreType.DMA((n + 1,)),
            pltpu.SemaphoreType.DMA((n,)),
        ],
        compiler_params=pltpu.CompilerParams(vmem_limit_bytes=vmem_mib * 1024 * 1024),
        cost_estimate=pl.CostEstimate(
            flops=2 * width * cols * rows * n * (2 if acc is None else 1),
            bytes_accessed=sum(map(size, pieces)) + size(grad_all) + width * cols * 8,
            transcendentals=0,
        ),
    )(places, *pieces, grad_all, *extra)


def per_device(activations, act_basis, gradients, grad_basis):
    xl, y, c = (lax.axis_index(a) for a in ("xl", "y", "c"))
    rows, act_width = activations.shape

    grad_rot = jnp.dot(gradients, grad_basis, preferred_element_type=jnp.float32)
    grad_sq = (grad_rot * grad_rot).astype(jnp.bfloat16)
    own = transpose_chips(grad_sq)

    act_blocks = activations.reshape(rows, act_width // BLOCK, BLOCK)
    act_rot = jnp.einsum("tbk,bkj->bjt", act_blocks, act_basis, preferred_element_type=jnp.float32)
    act_sq = (act_rot * act_rot).astype(jnp.bfloat16).reshape(act_width, rows)
    near_up, near_down = [act_sq], [act_sq]
    for _ in range(3):
        near_up.append(shift(near_up[-1], "y", Y, 1))
        near_down.append(shift(near_down[-1], "y", Y, -1))
    near_up.append(shift(near_up[-1], "y", Y, 1))
    far_up = [shift(act_sq, "xl", XL, 1)]
    far_down = far_up[:]
    for _ in range(3):
        far_up.append(shift(far_up[-1], "y", Y, 1))
        far_down.append(shift(far_down[-1], "y", Y, -1))
    far_down.append(shift(far_down[-1], "y", Y, -1))

    own, _ = lax.optimization_barrier((own, near_up[1]))
    copies = jnp.broadcast_to(own, (XH * Z,) + own.shape)
    grad_all = lax.all_to_all(copies, ("xh", "z"), 0, 0, tiled=True)
    grad_all = grad_all.reshape(XH * Z, rows, gradients.shape[1])

    pieces, at = [], []
    for k in range(5):
        for way, ring, pair in ((-1, near_up, 0), (1, near_down, 0), (-1, far_up, 1), (1, far_down, 1)):
            if k < len(ring) and (k > 0 or way < 0):
                pieces.append(ring[k])
                at.append((pair ^ xl) * Y + (y + Y + way * k) % Y)

    early = len(pieces) - 2
    first = products(jnp.stack(at[:early]).astype(jnp.int32), pieces[:early], grad_all)

    def rest(half):
        return products(jnp.stack(at[early:] + [half]).astype(jnp.int32), pieces[early:], grad_all, first)

    other = rest(1 - c)
    got = shift(other, "c", C, 1)
    return (rest(c) + got) / TOKENS


def solution(mesh):
    chips = Mesh(mesh.devices.reshape(XH, Z, XL, Y, C), ("xh", "z", "xl", "y", "c"))
    feat, tok = ("xh", "z"), ("xl", "y", "c")
    return jax.shard_map(
        per_device,
        mesh=chips,
        in_specs=(P(tok, feat), P(feat, None, None), P(tok, feat), P(feat, None)),
        out_specs=P(feat, tok),
        check_vma=False,
    )
```

```python
import jax
import jax.numpy as jnp
from jax import lax
from jax.experimental import pallas as pl
from jax.experimental.pallas import tpu as pltpu
from jax.sharding import Mesh
from jax.sharding import PartitionSpec as P

BLOCK = 512
TOKENS = 4096
XH, Z, XL, Y, C = 2, 8, 2, 8, 2


def transpose_chips(x, sent):
    chips = XH * Z
    swaps = [[f * chips + m, m * chips + f] for f in range(chips) for m in range(f + 1, chips)]
    fixed = [f * chips + f for f in range(chips)]
    groups = swaps + [[fixed[i], fixed[i + 1]] for i in range(0, chips, 2)]
    f = lax.axis_index("xh") * Z + lax.axis_index("z")
    m = lax.axis_index("xl") * Y + lax.axis_index("y")
    got = lax.all_to_all(sent, ("xh", "z", "xl", "y"), 0, 0, axis_index_groups=groups)
    return jnp.where(f > m, got[0], jnp.where(f < m, got[1], x))


def swap(x, axis):
    return lax.ppermute(x, axis, [(0, 1), (1, 0)])


def product(swapped, act_all, near, far):
    _, _, width, rows = act_all.shape
    cols = near.shape[2]
    tile = width // 2

    def kernel(swapped_ref, act_ref, near_ref, far_ref, out_ref):
        def go(blocks):
            for t in range(width // tile):
                at = slice(t * tile, (t + 1) * tile)
                total = None
                for pair in range(2):
                    act = jnp.concatenate([act_ref[y, pair, at] for y in range(Y)], axis=1)
                    grad = jnp.concatenate([blocks[pair][y] for y in range(Y)], axis=0)
                    part = jnp.dot(act, grad, preferred_element_type=jnp.float32)
                    total = part if total is None else total + part
                out_ref[at] = total

        @pl.when(swapped_ref[0] == 0)
        def _():
            go((near_ref, far_ref))

        @pl.when(swapped_ref[0] != 0)
        def _():
            go((far_ref, near_ref))

    vmem = pl.BlockSpec(memory_space=pltpu.VMEM)
    return pl.pallas_call(
        kernel,
        in_specs=[pl.BlockSpec(memory_space=pltpu.SMEM), vmem, vmem, vmem],
        out_specs=vmem,
        out_shape=jax.ShapeDtypeStruct((width, cols), jnp.float32),
        compiler_params=pltpu.CompilerParams(vmem_limit_bytes=16 * 1024 * 1024),
        cost_estimate=pl.CostEstimate(
            flops=2 * width * cols * rows * 2 * Y,
            bytes_accessed=act_all.size * 2 + near.size * 4 + width * cols * 4,
            transcendentals=0,
        ),
    )(swapped, act_all, near, far)


def per_device(activations, act_basis, gradients, grad_basis):
    rows, act_width = activations.shape
    xh, c = lax.axis_index("xh"), lax.axis_index("c")

    grad_rot = jnp.dot(gradients, grad_basis, preferred_element_type=jnp.float32)
    grad_sq = (grad_rot * grad_rot).astype(jnp.bfloat16)
    grad_pair = jnp.broadcast_to(grad_sq, (2,) + grad_sq.shape)
    own = transpose_chips(grad_sq, grad_pair)

    act_blocks = activations.reshape(rows, act_width // BLOCK, BLOCK)
    act_rot = jnp.einsum("tbk,bkj->bjt", act_blocks, act_basis, preferred_element_type=jnp.float32)
    act_sq = (act_rot * act_rot).astype(jnp.bfloat16).reshape(act_width, rows)
    act_pair = lax.all_gather(act_sq, "xl", axis=0)
    act_pair, _ = lax.optimization_barrier((act_pair, own))
    act_all = lax.all_gather(act_pair, "y", axis=0)

    def gathered(half):
        cols = own.shape[1] // 2
        mine = lax.dynamic_slice_in_dim(own, half * cols, cols, 1)
        near = lax.all_to_all(jnp.broadcast_to(mine, (Z,) + mine.shape), "z", 0, 0)
        return near, swap(near, "xh")

    swapped = xh[None]
    theirs, ours = gathered(1 - c), gathered(c)
    act_all, _ = lax.optimization_barrier((act_all, ours))
    other = product(swapped, act_all, *theirs)
    got = swap(other, "c")
    mine = product(swapped, act_all, *ours)
    return (mine + got) / TOKENS


def solution(mesh):
    chips = Mesh(mesh.devices.reshape(XH, Z, XL, Y, C), ("xh", "z", "xl", "y", "c"))
    feat, tok = ("xh", "z"), ("xl", "y", "c")
    return jax.shard_map(
        per_device,
        mesh=chips,
        in_specs=(P(tok, feat), P(feat, None, None), P(tok, feat), P(feat, None)),
        out_specs=P(feat, tok),
        check_vma=False,
    )
```

```python
import jax
import jax.numpy as jnp
from jax import lax
from jax.experimental import pallas as pl
from jax.experimental.pallas import tpu as pltpu
from jax.sharding import Mesh
from jax.sharding import PartitionSpec as P

BLOCK = 512
TOKENS = 4096
XH, Z, XL, Y, C = 2, 8, 2, 8, 2


def transpose_chips(x, sent):
    chips = XH * Z
    swaps = [[f * chips + m, m * chips + f] for f in range(chips) for m in range(f + 1, chips)]
    fixed = [f * chips + f for f in range(chips)]
    groups = swaps + [[fixed[i], fixed[i + 1]] for i in range(0, chips, 2)]
    f = lax.axis_index("xh") * Z + lax.axis_index("z")
    m = lax.axis_index("xl") * Y + lax.axis_index("y")
    got = lax.all_to_all(sent, ("xh", "z", "xl", "y"), 0, 0, axis_index_groups=groups)
    return jnp.where(f > m, got[0], jnp.where(f < m, got[1], x))


def swap(x, axis):
    return lax.ppermute(x, axis, [(0, 1), (1, 0)])


def shift(x, axis, size, step):
    return lax.ppermute(x, axis, [(i, (i + step) % size) for i in range(size)])


def product(places, act_all, sides, near, far):
    rest, rows = sides[0].shape
    width = act_all.shape[1] - rest
    cols = near.shape[2] // 2
    tile = width // 2

    def kernel(places_ref, act_ref, *refs):
        side_refs, (near_ref, far_ref, out_ref) = refs[:Y], refs[Y:]
        where = pl.ds(pl.multiple_of(places_ref[1] * cols, cols), cols)

        def go(own_ref, other_ref):
            own = jnp.concatenate([own_ref[y, :, where] for y in range(Y)], axis=0)
            other = jnp.concatenate([other_ref[y, :, where] for y in range(Y)], axis=0)
            for t in range(2):
                at = slice(t * tile, (t + 1) * tile)
                lhs = jnp.concatenate([act_ref[y, at] for y in range(Y)], axis=1)
                total = jnp.dot(lhs, own, preferred_element_type=jnp.float32)
                if t == 0:
                    lhs = jnp.concatenate([act_ref[y, width:] for y in range(Y)], axis=1)
                else:
                    lhs = jnp.concatenate([ref[...] for ref in side_refs], axis=1)
                    other = jnp.concatenate([other_ref[places_ref[2 + d], :, where] for d in range(Y)], axis=0)
                out_ref[at] = total + jnp.dot(lhs, other, preferred_element_type=jnp.float32)

        @pl.when(places_ref[0] == 0)
        def _():
            go(near_ref, far_ref)

        @pl.when(places_ref[0] != 0)
        def _():
            go(far_ref, near_ref)

    vmem = pl.BlockSpec(memory_space=pltpu.VMEM)
    return pl.pallas_call(
        kernel,
        in_specs=[pl.BlockSpec(memory_space=pltpu.SMEM)] + [vmem] * (Y + 3),
        out_specs=vmem,
        out_shape=jax.ShapeDtypeStruct((width, cols), jnp.float32),
        compiler_params=pltpu.CompilerParams(vmem_limit_bytes=16 * 1024 * 1024),
        cost_estimate=pl.CostEstimate(
            flops=2 * width * cols * rows * 2 * Y,
            bytes_accessed=(act_all.size + rest * rows * Y + near.size * 2) * 2 + width * cols * 4,
            transcendentals=0,
        ),
    )(places, act_all, *sides, near, far)


def per_device(activations, act_basis, gradients, grad_basis):
    rows, act_width = activations.shape
    xh, y, c = (lax.axis_index(a) for a in ("xh", "y", "c"))

    grad_rot = jnp.dot(gradients, grad_basis, preferred_element_type=jnp.float32)
    grad_sq = (grad_rot * grad_rot).astype(jnp.bfloat16)
    grad_pair = jnp.broadcast_to(grad_sq, (2,) + grad_sq.shape)
    own = transpose_chips(grad_sq, grad_pair)

    act_blocks = activations.reshape(rows, act_width // BLOCK, BLOCK)
    act_rot = jnp.einsum("tbk,bkj->bjt", act_blocks, act_basis, preferred_element_type=jnp.float32)
    act_sq = (act_rot * act_rot).astype(jnp.bfloat16).reshape(act_width, rows)
    act_pair = lax.all_gather(act_sq, "xl", axis=0, tiled=True)
    split = act_pair.shape[0] * 3 // 4
    sent, _ = lax.optimization_barrier((act_pair[:split], own))
    act_all = lax.all_gather(sent, "y", axis=0)

    near = lax.all_to_all(jnp.broadcast_to(own, (Z,) + own.shape), "z", 0, 0)
    sides = [act_pair[split:]]
    sides += [shift(sides[0], "y", Y, d) for d in (1, 7, 2, 6, 3, 5, 4)]
    near, _ = lax.optimization_barrier((near, sides[1:5]))
    far = swap(near, "xh")
    side_y = [(y + Y - d) % Y for d in (0, 1, 7, 2, 6, 3, 5, 4)]

    def places(half):
        return jnp.stack([xh, half] + side_y).astype(jnp.int32)

    other = product(places(1 - c), act_all, sides, near, far)
    got = swap(other, "c")
    mine = product(places(c), act_all, sides, near, far)
    return (mine + got) / TOKENS


def solution(mesh):
    chips = Mesh(mesh.devices.reshape(XH, Z, XL, Y, C), ("xh", "z", "xl", "y", "c"))
    feat, tok = ("xh", "z"), ("xl", "y", "c")
    return jax.shard_map(
        per_device,
        mesh=chips,
        in_specs=(P(tok, feat), P(feat, None, None), P(tok, feat), P(feat, None)),
        out_specs=P(feat, tok),
        check_vma=False,
    )
```

```python
import jax
import jax.numpy as jnp
from jax import lax
from jax.experimental import pallas as pl
from jax.experimental.pallas import tpu as pltpu
from jax.sharding import Mesh
from jax.sharding import PartitionSpec as P

BLOCK = 512
TOKENS = 4096
XH, Z, XL, Y, C = 2, 8, 2, 8, 2


def shift(x, axis, size, step):
    return lax.ppermute(x, axis, [(i, (i + step) % size) for i in range(size)])


def transpose_chips(x):
    chips = XH * Z
    swaps = [[f * chips + m, m * chips + f] for f in range(chips) for m in range(f + 1, chips)]
    fixed = [f * chips + f for f in range(chips)]
    groups = swaps + [[fixed[i], fixed[i + 1]] for i in range(0, chips, 2)]
    f = lax.axis_index("xh") * Z + lax.axis_index("z")
    m = lax.axis_index("xl") * Y + lax.axis_index("y")
    sent = jnp.broadcast_to(x, (2,) + x.shape)
    got = lax.all_to_all(sent, ("xh", "z", "xl", "y"), 0, 0, axis_index_groups=groups)
    return jnp.where(f > m, got[0], jnp.where(f < m, got[1], x))


def products(places, pieces, near, far):
    width, rows = pieces[0].shape
    cols = near.shape[2] // 2
    n = len(pieces)
    tile = width // 2
    per_group = 4

    def kernel(places_ref, *refs):
        piece_refs, (near_ref, far_ref, out_ref, held, grads, sems, grad_sems) = refs[:n], refs[n:]
        where = pl.ds(pl.multiple_of(places_ref[1] * cols, cols), cols)
        grad_copies = [
            pltpu.make_async_copy(ref.at[:, :, where], grads.at[i], grad_sems.at[i])
            for i, ref in enumerate((near_ref, far_ref))
        ]
        for copy in grad_copies:
            copy.start()
        copies = [pltpu.make_async_copy(piece_refs[i], held.at[i], sems.at[i]) for i in range(n)]
        for copy in copies:
            copy.start()
        for copy in grad_copies:
            copy.wait()
        for first in range(0, n, per_group):
            group = range(first, first + per_group)
            grad = jnp.concatenate([grads[(i % 2) ^ places_ref[0], places_ref[2 + i]] for i in group], axis=0)
            for i in group:
                copies[i].wait()
            for t in range(width // tile):
                at = slice(t * tile, (t + 1) * tile)
                lhs = jnp.concatenate([held[i, at] for i in group], axis=1)
                total = jnp.dot(lhs, grad, preferred_element_type=jnp.float32)
                if first == 0:
                    out_ref[at] = total
                else:
                    out_ref[at] += total

    def size(a):
        return a.size * a.dtype.itemsize

    hbm = pl.BlockSpec(memory_space=pltpu.HBM)
    return pl.pallas_call(
        kernel,
        in_specs=[pl.BlockSpec(memory_space=pltpu.SMEM)] + [hbm] * (n + 2),
        out_specs=pl.BlockSpec(memory_space=pltpu.VMEM),
        out_shape=jax.ShapeDtypeStruct((width, cols), jnp.float32),
        scratch_shapes=[
            pltpu.VMEM((n, width, rows), pieces[0].dtype),
            pltpu.VMEM((2,) + near.shape[:2] + (cols,), near.dtype),
            pltpu.SemaphoreType.DMA((n,)),
            pltpu.SemaphoreType.DMA((2,)),
        ],
        compiler_params=pltpu.CompilerParams(vmem_limit_bytes=56 * 1024 * 1024),
        cost_estimate=pl.CostEstimate(
            flops=2 * width * cols * rows * n,
            bytes_accessed=sum(map(size, pieces)) + size(near) + width * cols * 4,
            transcendentals=0,
        ),
    )(places, *pieces, near, far)


def per_device(activations, act_basis, gradients, grad_basis):
    xh, xl, y, c = (lax.axis_index(a) for a in ("xh", "xl", "y", "c"))
    rows, act_width = activations.shape

    grad_rot = jnp.dot(gradients, grad_basis, preferred_element_type=jnp.float32)
    grad_sq = (grad_rot * grad_rot).astype(jnp.bfloat16)
    own = transpose_chips(grad_sq)

    act_blocks = activations.reshape(rows, act_width // BLOCK, BLOCK)
    act_rot = jnp.einsum("tbk,bkj->bjt", act_blocks, act_basis, preferred_element_type=jnp.float32)
    act_sq = (act_rot * act_rot).astype(jnp.bfloat16).reshape(act_width, rows)
    near_up, near_down = [act_sq], [act_sq]
    far_up = [shift(act_sq, "xl", XL, 1)]
    far_down = far_up[:]
    near_up.append(shift(act_sq, "y", Y, 1))
    near_down.append(shift(act_sq, "y", Y, -1))
    own, _ = lax.optimization_barrier((own, (near_up[1], near_down[1], far_up[0])))
    near = lax.all_to_all(jnp.broadcast_to(own, (Z,) + own.shape), "z", 0, 0)
    for k in range(1, 4):
        far_up.append(shift(far_up[-1], "y", Y, 1))
        far_down.append(shift(far_down[-1], "y", Y, -1))
        near_up.append(shift(near_up[-1], "y", Y, 1))
        if k < 3:
            near_down.append(shift(near_down[-1], "y", Y, -1))
    far_down.append(shift(far_down[-1], "y", Y, -1))

    near, _ = lax.optimization_barrier((near, (near_up[2], near_down[2], far_up[1], far_down[1])))
    far = shift(near, "xh", XH, 1)

    pieces, at = [near_up[0], far_up[0]], [y, y]
    for k in range(1, 4):
        pieces += [near_up[k], far_up[k], near_down[k], far_down[k]]
        at += [(y + Y - k) % Y] * 2 + [(y + k) % Y] * 2
    pieces += [near_up[4], far_down[4]]
    at += [(y + 4) % Y] * 2

    def places(half):
        return jnp.stack([xh ^ xl, half] + at).astype(jnp.int32)

    other = products(places(1 - c), pieces, near, far)
    got = shift(other, "c", C, 1)
    mine = products(places(c), pieces, near, far)
    return (mine + got) / TOKENS


def solution(mesh):
    chips = Mesh(mesh.devices.reshape(XH, Z, XL, Y, C), ("xh", "z", "xl", "y", "c"))
    feat, tok = ("xh", "z"), ("xl", "y", "c")
    return jax.shard_map(
        per_device,
        mesh=chips,
        in_specs=(P(tok, feat), P(feat, None, None), P(tok, feat), P(feat, None)),
        out_specs=P(feat, tok),
        check_vma=False,
    )
```

```python
import jax
import jax.numpy as jnp
from jax import lax
from jax.experimental import pallas as pl
from jax.experimental.pallas import tpu as pltpu
from jax.sharding import Mesh
from jax.sharding import PartitionSpec as P

BLOCK = 512
TOKENS = 4096
XH, Z, XL, Y, C = 2, 8, 2, 8, 2


def transpose_chips(x, sent):
    chips = XH * Z
    swaps = [[f * chips + m, m * chips + f] for f in range(chips) for m in range(f + 1, chips)]
    fixed = [f * chips + f for f in range(chips)]
    groups = swaps + [[fixed[i], fixed[i + 1]] for i in range(0, chips, 2)]
    f = lax.axis_index("xh") * Z + lax.axis_index("z")
    m = lax.axis_index("xl") * Y + lax.axis_index("y")
    got = lax.all_to_all(sent, ("xh", "z", "xl", "y"), 0, 0, axis_index_groups=groups)
    return jnp.where(f > m, got[0], jnp.where(f < m, got[1], x))


def swap(x, axis):
    return lax.ppermute(x, axis, [(0, 1), (1, 0)])


def product(swapped, act_all, near, far, parts):
    _, _, width, rows = act_all.shape
    cols = near.shape[2]
    tile = width // 2

    def kernel(swapped_ref, act_ref, near_ref, far_ref, *out_refs):
        def go(blocks):
            for t in range(width // tile):
                at = slice(t * tile, (t + 1) * tile)
                total = None
                for pair in range(2):
                    act = jnp.concatenate([act_ref[y, pair, at] for y in range(Y)], axis=1)
                    grad = jnp.concatenate([blocks[pair][y] for y in range(Y)], axis=0)
                    part = jnp.dot(act, grad, preferred_element_type=jnp.float32)
                    total = part if total is None else total + part
                if parts == 1:
                    out_refs[0][at] = total
                else:
                    out_refs[t][...] = total

        @pl.when(swapped_ref[0] == 0)
        def _():
            go((near_ref, far_ref))

        @pl.when(swapped_ref[0] != 0)
        def _():
            go((far_ref, near_ref))

    vmem = pl.BlockSpec(memory_space=pltpu.VMEM)
    return pl.pallas_call(
        kernel,
        in_specs=[pl.BlockSpec(memory_space=pltpu.SMEM), vmem, vmem, vmem],
        out_specs=[vmem] * parts,
        out_shape=[jax.ShapeDtypeStruct((width // parts, cols), jnp.float32)] * parts,
        compiler_params=pltpu.CompilerParams(vmem_limit_bytes=16 * 1024 * 1024),
        cost_estimate=pl.CostEstimate(
            flops=2 * width * cols * rows * 2 * Y,
            bytes_accessed=act_all.size * 2 + near.size * 4 + width * cols * 4,
            transcendentals=0,
        ),
    )(swapped, act_all, near, far)


def per_device(activations, act_basis, gradients, grad_basis):
    rows, act_width = activations.shape
    xh, c = lax.axis_index("xh"), lax.axis_index("c")

    grad_rot = jnp.dot(gradients, grad_basis, preferred_element_type=jnp.float32)
    grad_sq = (grad_rot * grad_rot).astype(jnp.bfloat16)
    grad_pair = jnp.broadcast_to(grad_sq, (2,) + grad_sq.shape)
    own = transpose_chips(grad_sq, grad_pair)

    activations, _ = lax.optimization_barrier((activations, grad_pair))
    act_blocks = activations.reshape(rows, act_width // BLOCK, BLOCK)
    act_rot = jnp.einsum("tbk,bkj->bjt", act_blocks, act_basis, preferred_element_type=jnp.float32)
    act_sq = (act_rot * act_rot).astype(jnp.bfloat16).reshape(act_width, rows)
    act_pair = lax.all_gather(act_sq, "xl", axis=0)
    act_all = lax.all_gather(act_pair, "y", axis=0)

    cols = own.shape[1] // 2

    def gathered(half):
        mine = lax.dynamic_slice_in_dim(own, half * cols, cols, 1)
        return lax.all_to_all(jnp.broadcast_to(mine, (Z,) + mine.shape), "z", 0, 0)

    near_other, near_mine = gathered(1 - c), gathered(c)
    far_other = swap(near_other, "xh")
    far_mine = swap(near_mine, "xh")
    swapped = xh[None]
    act_all, _ = lax.optimization_barrier((act_all, near_mine))
    other = product(swapped, act_all, near_other, far_other, 2)
    got = [swap(part, "c") for part in other]
    (mine,) = product(swapped, act_all, near_mine, far_mine, 1)
    return (mine + jnp.concatenate(got)) / TOKENS


def solution(mesh):
    chips = Mesh(mesh.devices.reshape(XH, Z, XL, Y, C), ("xh", "z", "xl", "y", "c"))
    feat, tok = ("xh", "z"), ("xl", "y", "c")
    return jax.shard_map(
        per_device,
        mesh=chips,
        in_specs=(P(tok, feat), P(feat, None, None), P(tok, feat), P(feat, None)),
        out_specs=P(feat, tok),
        check_vma=False,
    )
```

```python
import jax
import jax.numpy as jnp
from jax import lax
from jax.experimental import pallas as pl
from jax.experimental.pallas import tpu as pltpu
from jax.sharding import Mesh
from jax.sharding import PartitionSpec as P

BLOCK = 512
TOKENS = 4096
XH, Z, XL, Y, C = 2, 8, 2, 8, 2


def transpose_chips(x, sent):
    chips = XH * Z
    swaps = [[f * chips + m, m * chips + f] for f in range(chips) for m in range(f + 1, chips)]
    fixed = [f * chips + f for f in range(chips)]
    groups = swaps + [[fixed[i], fixed[i + 1]] for i in range(0, chips, 2)]
    f = lax.axis_index("xh") * Z + lax.axis_index("z")
    m = lax.axis_index("xl") * Y + lax.axis_index("y")
    got = lax.all_to_all(sent, ("xh", "z", "xl", "y"), 0, 0, axis_index_groups=groups)
    return jnp.where(f > m, got[0], jnp.where(f < m, got[1], x))


def swap(x, axis):
    return lax.ppermute(x, axis, [(0, 1), (1, 0)])


def product(swapped, act_all, near, far, parts):
    _, _, width, rows = act_all.shape
    cols = near.shape[2]
    tile = width // 2

    def kernel(swapped_ref, act_ref, near_ref, far_ref, *out_refs):
        def go(blocks):
            for t in range(width // tile):
                at = slice(t * tile, (t + 1) * tile)
                total = None
                for pair in range(2):
                    act = jnp.concatenate([act_ref[y, pair, at] for y in range(Y)], axis=1)
                    grad = jnp.concatenate([blocks[pair][y] for y in range(Y)], axis=0)
                    part = jnp.dot(act, grad, preferred_element_type=jnp.float32)
                    total = part if total is None else total + part
                if parts == 1:
                    out_refs[0][at] = total
                else:
                    out_refs[t][...] = total

        @pl.when(swapped_ref[0] == 0)
        def _():
            go((near_ref, far_ref))

        @pl.when(swapped_ref[0] != 0)
        def _():
            go((far_ref, near_ref))

    vmem = pl.BlockSpec(memory_space=pltpu.VMEM)
    return pl.pallas_call(
        kernel,
        in_specs=[pl.BlockSpec(memory_space=pltpu.SMEM), vmem, vmem, vmem],
        out_specs=[vmem] * parts,
        out_shape=[jax.ShapeDtypeStruct((width // parts, cols), jnp.float32)] * parts,
        compiler_params=pltpu.CompilerParams(vmem_limit_bytes=16 * 1024 * 1024),
        cost_estimate=pl.CostEstimate(
            flops=2 * width * cols * rows * 2 * Y,
            bytes_accessed=act_all.size * 2 + near.size * 4 + width * cols * 4,
            transcendentals=0,
        ),
    )(swapped, act_all, near, far)


def copies(x, count):
    def kernel(x_ref, out_ref):
        out_ref[...] = jnp.broadcast_to(x_ref[...][None], out_ref.shape)

    vmem = pl.BlockSpec(memory_space=pltpu.VMEM)
    return pl.pallas_call(
        kernel,
        in_specs=[vmem],
        out_specs=vmem,
        out_shape=jax.ShapeDtypeStruct((count,) + x.shape, x.dtype),
        compiler_params=pltpu.CompilerParams(vmem_limit_bytes=16 * 1024 * 1024),
        cost_estimate=pl.CostEstimate(flops=100_000_000_000, bytes_accessed=(count + 1) * x.size * 2, transcendentals=0),
    )(x)


def per_device(activations, act_basis, gradients, grad_basis):
    rows, act_width = activations.shape
    xh, c = lax.axis_index("xh"), lax.axis_index("c")

    grad_rot = jnp.dot(gradients, grad_basis, preferred_element_type=jnp.float32)
    grad_sq = (grad_rot * grad_rot).astype(jnp.bfloat16)
    grad_pair = jnp.broadcast_to(grad_sq, (2,) + grad_sq.shape)
    own = transpose_chips(grad_sq, grad_pair)

    act_blocks = activations.reshape(rows, act_width // BLOCK, BLOCK)
    act_rot = jnp.einsum("tbk,bkj->bjt", act_blocks, act_basis, preferred_element_type=jnp.float32)
    act_sq = (act_rot * act_rot).astype(jnp.bfloat16).reshape(act_width, rows)
    act_pair = lax.all_gather(act_sq, "xl", axis=0)
    act_all = lax.all_gather(act_pair, "y", axis=0)

    cols = own.shape[1] // 2

    def gathered(half):
        mine = lax.dynamic_slice_in_dim(own, half * cols, cols, 1)
        return lax.all_to_all(copies(mine, Z), "z", 0, 0)

    near_other, near_mine = gathered(1 - c), gathered(c)
    far_other = swap(near_other, "xh")
    far_mine = swap(near_mine, "xh")
    swapped = xh[None]
    act_all, _ = lax.optimization_barrier((act_all, near_mine))
    other = product(swapped, act_all, near_other, far_other, 2)
    got = [swap(part, "c") for part in other]
    (mine,) = product(swapped, act_all, near_mine, far_mine, 1)
    return (mine + jnp.concatenate(got)) / TOKENS


def solution(mesh):
    chips = Mesh(mesh.devices.reshape(XH, Z, XL, Y, C), ("xh", "z", "xl", "y", "c"))
    feat, tok = ("xh", "z"), ("xl", "y", "c")
    return jax.shard_map(
        per_device,
        mesh=chips,
        in_specs=(P(tok, feat), P(feat, None, None), P(tok, feat), P(feat, None)),
        out_specs=P(feat, tok),
        check_vma=False,
    )
```

```python
import jax
import jax.numpy as jnp
from jax import lax
from jax.experimental import pallas as pl
from jax.experimental.pallas import tpu as pltpu
from jax.sharding import Mesh
from jax.sharding import PartitionSpec as P

BLOCK = 512
TOKENS = 4096
XH, Z, XL, Y, C = 2, 8, 2, 8, 2


def transpose_chips(x, sent):
    chips = XH * Z
    swaps = [[f * chips + m, m * chips + f] for f in range(chips) for m in range(f + 1, chips)]
    fixed = [f * chips + f for f in range(chips)]
    groups = swaps + [[fixed[i], fixed[i + 1]] for i in range(0, chips, 2)]
    f = lax.axis_index("xh") * Z + lax.axis_index("z")
    m = lax.axis_index("xl") * Y + lax.axis_index("y")
    got = lax.all_to_all(sent, ("xh", "z", "xl", "y"), 0, 0, axis_index_groups=groups)
    return jnp.where(f > m, got[0], jnp.where(f < m, got[1], x))


def swap(x, axis):
    return lax.ppermute(x, axis, [(0, 1), (1, 0)])


def product(swapped, act_all, near, far, parts):
    _, _, width, rows = act_all.shape
    cols = near.shape[2]
    tile = width // 2

    def kernel(swapped_ref, act_ref, near_ref, far_ref, *out_refs):
        def go(blocks):
            for t in range(width // tile):
                at = slice(t * tile, (t + 1) * tile)
                total = None
                for pair in range(2):
                    act = jnp.concatenate([act_ref[y, pair, at] for y in range(Y)], axis=1)
                    grad = jnp.concatenate([blocks[pair][y] for y in range(Y)], axis=0)
                    part = jnp.dot(act, grad, preferred_element_type=jnp.float32)
                    total = part if total is None else total + part
                if parts == 1:
                    out_refs[0][at] = total
                else:
                    out_refs[t][...] = total

        @pl.when(swapped_ref[0] == 0)
        def _():
            go((near_ref, far_ref))

        @pl.when(swapped_ref[0] != 0)
        def _():
            go((far_ref, near_ref))

    vmem = pl.BlockSpec(memory_space=pltpu.VMEM)
    return pl.pallas_call(
        kernel,
        in_specs=[pl.BlockSpec(memory_space=pltpu.SMEM), vmem, vmem, vmem],
        out_specs=[vmem] * parts,
        out_shape=[jax.ShapeDtypeStruct((width // parts, cols), jnp.float32)] * parts,
        compiler_params=pltpu.CompilerParams(vmem_limit_bytes=16 * 1024 * 1024),
        cost_estimate=pl.CostEstimate(
            flops=2 * width * cols * rows * 2 * Y,
            bytes_accessed=act_all.size * 2 + near.size * 4 + width * cols * 4,
            transcendentals=0,
        ),
    )(swapped, act_all, near, far)


def copies(x, count):
    def kernel(x_ref, out_ref):
        out_ref[...] = jnp.broadcast_to(x_ref[...][None], out_ref.shape)

    vmem = pl.BlockSpec(memory_space=pltpu.VMEM)
    return pl.pallas_call(
        kernel,
        in_specs=[vmem],
        out_specs=vmem,
        out_shape=jax.ShapeDtypeStruct((count,) + x.shape, x.dtype),
        compiler_params=pltpu.CompilerParams(vmem_limit_bytes=16 * 1024 * 1024),
        cost_estimate=pl.CostEstimate(flops=50_000_000_000, bytes_accessed=(count + 1) * x.size * 2, transcendentals=0),
    )(x)


def per_device(activations, act_basis, gradients, grad_basis):
    rows, act_width = activations.shape
    xh, xl, c = (lax.axis_index(a) for a in ("xh", "xl", "c"))

    act_blocks = activations.reshape(rows, act_width // BLOCK, BLOCK)
    act_rot = jnp.einsum("tbk,bkj->bjt", act_blocks, act_basis, preferred_element_type=jnp.float32)
    act_sq = (act_rot * act_rot).astype(jnp.bfloat16).reshape(act_width, rows)

    gradients, _ = lax.optimization_barrier((gradients, act_sq))
    grad_rot = jnp.dot(gradients, grad_basis, preferred_element_type=jnp.float32)
    grad_sq = (grad_rot * grad_rot).astype(jnp.bfloat16)
    grad_pair = jnp.broadcast_to(grad_sq, (2,) + grad_sq.shape)
    own = transpose_chips(grad_sq, grad_pair)

    act_pair = jnp.stack([act_sq, swap(act_sq, "xl")])
    act_all = lax.all_gather(act_pair, "y", axis=0)

    cols = own.shape[1] // 2

    def gathered(half):
        mine = lax.dynamic_slice_in_dim(own, half * cols, cols, 1)
        return lax.all_to_all(copies(mine, Z), "z", 0, 0)

    near_other, near_mine = gathered(1 - c), gathered(c)
    far_other = swap(near_other, "xh")
    far_mine = swap(near_mine, "xh")
    swapped = (xh ^ xl)[None]
    act_all, _ = lax.optimization_barrier((act_all, near_mine))
    other = product(swapped, act_all, near_other, far_other, 2)
    got = [swap(part, "c") for part in other]
    (mine,) = product(swapped, act_all, near_mine, far_mine, 1)
    return (mine + jnp.concatenate(got)) / TOKENS


def solution(mesh):
    chips = Mesh(mesh.devices.reshape(XH, Z, XL, Y, C), ("xh", "z", "xl", "y", "c"))
    feat, tok = ("xh", "z"), ("xl", "y", "c")
    return jax.shard_map(
        per_device,
        mesh=chips,
        in_specs=(P(tok, feat), P(feat, None, None), P(tok, feat), P(feat, None)),
        out_specs=P(feat, tok),
        check_vma=False,
    )
```

```python
import jax
import jax.numpy as jnp
from jax import lax
from jax.experimental import pallas as pl
from jax.experimental.pallas import tpu as pltpu
from jax.sharding import Mesh
from jax.sharding import PartitionSpec as P

BLOCK = 512
TOKENS = 4096
XH, Z, XL, Y, C = 2, 8, 2, 8, 2


def transpose_chips(x, sent):
    chips = XH * Z
    swaps = [[f * chips + m, m * chips + f] for f in range(chips) for m in range(f + 1, chips)]
    fixed = [f * chips + f for f in range(chips)]
    groups = swaps + [[fixed[i], fixed[i + 1]] for i in range(0, chips, 2)]
    f = lax.axis_index("xh") * Z + lax.axis_index("z")
    m = lax.axis_index("xl") * Y + lax.axis_index("y")
    got = lax.all_to_all(sent, ("xh", "z", "xl", "y"), 0, 0, axis_index_groups=groups)
    return jnp.where(f > m, got[0], jnp.where(f < m, got[1], x))


def swap(x, axis):
    return lax.ppermute(x, axis, [(0, 1), (1, 0)])


def product(swapped, act_all, near, far, parts):
    _, _, width, rows = act_all.shape
    cols = near.shape[2]
    tile = width // 2

    def kernel(swapped_ref, act_ref, near_ref, far_ref, *out_refs):
        def go(blocks):
            for t in range(width // tile):
                at = slice(t * tile, (t + 1) * tile)
                total = None
                for pair in range(2):
                    act = jnp.concatenate([act_ref[y, pair, at] for y in range(Y)], axis=1)
                    grad = jnp.concatenate([blocks[pair][y] for y in range(Y)], axis=0)
                    part = jnp.dot(act, grad, preferred_element_type=jnp.float32)
                    total = part if total is None else total + part
                if parts == 1:
                    out_refs[0][at] = total
                else:
                    out_refs[t][...] = total

        @pl.when(swapped_ref[0] == 0)
        def _():
            go((near_ref, far_ref))

        @pl.when(swapped_ref[0] != 0)
        def _():
            go((far_ref, near_ref))

    vmem = pl.BlockSpec(memory_space=pltpu.VMEM)
    return pl.pallas_call(
        kernel,
        in_specs=[pl.BlockSpec(memory_space=pltpu.SMEM), vmem, vmem, vmem],
        out_specs=[vmem] * parts,
        out_shape=[jax.ShapeDtypeStruct((width // parts, cols), jnp.float32)] * parts,
        compiler_params=pltpu.CompilerParams(vmem_limit_bytes=16 * 1024 * 1024),
        cost_estimate=pl.CostEstimate(
            flops=2 * width * cols * rows * 2 * Y,
            bytes_accessed=act_all.size * 2 + near.size * 4 + width * cols * 4,
            transcendentals=0,
        ),
    )(swapped, act_all, near, far)


def per_device(activations, act_basis, gradients, grad_basis):
    rows, act_width = activations.shape
    xh, xl, c = (lax.axis_index(a) for a in ("xh", "xl", "c"))

    grad_rot = jnp.dot(gradients, grad_basis, preferred_element_type=jnp.float32)
    grad_sq = (grad_rot * grad_rot).astype(jnp.bfloat16)
    grad_pair = jnp.broadcast_to(grad_sq, (2,) + grad_sq.shape)
    own = transpose_chips(grad_sq, grad_pair)

    def rotated(act):
        blocks = act.reshape(rows, act_width // BLOCK, BLOCK)
        rot = jnp.einsum("tbk,bkj->bjt", blocks, act_basis, preferred_element_type=jnp.float32)
        return (rot * rot).astype(jnp.bfloat16).reshape(act_width, rows)

    others, _ = lax.optimization_barrier((swap(activations, "xl"), grad_pair))
    act_pair = jnp.stack([rotated(activations), rotated(others)])
    act_all = lax.all_gather(act_pair, "y", axis=0)

    cols = own.shape[1] // 2

    def gathered(half):
        mine = lax.dynamic_slice_in_dim(own, half * cols, cols, 1)
        return lax.all_to_all(jnp.broadcast_to(mine, (Z,) + mine.shape), "z", 0, 0)

    near_other, near_mine = gathered(1 - c), gathered(c)
    far_other = swap(near_other, "xh")
    far_mine = swap(near_mine, "xh")
    swapped = (xh ^ xl)[None]
    act_all, _ = lax.optimization_barrier((act_all, near_mine))
    other = product(swapped, act_all, near_other, far_other, 2)
    got = [swap(part, "c") for part in other]
    (mine,) = product(swapped, act_all, near_mine, far_mine, 1)
    return (mine + jnp.concatenate(got)) / TOKENS


def solution(mesh):
    chips = Mesh(mesh.devices.reshape(XH, Z, XL, Y, C), ("xh", "z", "xl", "y", "c"))
    feat, tok = ("xh", "z"), ("xl", "y", "c")
    return jax.shard_map(
        per_device,
        mesh=chips,
        in_specs=(P(tok, feat), P(feat, None, None), P(tok, feat), P(feat, None)),
        out_specs=P(feat, tok),
        check_vma=False,
    )
```

```python
import jax
import jax.numpy as jnp
from jax import lax
from jax.experimental import pallas as pl
from jax.experimental.pallas import tpu as pltpu
from jax.sharding import Mesh
from jax.sharding import PartitionSpec as P

BLOCK = 512
TOKENS = 4096
XH, Z, XL, Y, C = 2, 8, 2, 8, 2


def transpose_chips(x, sent):
    chips = XH * Z
    swaps = [[f * chips + m, m * chips + f] for f in range(chips) for m in range(f + 1, chips)]
    fixed = [f * chips + f for f in range(chips)]
    groups = swaps + [[fixed[i], fixed[i + 1]] for i in range(0, chips, 2)]
    f = lax.axis_index("xh") * Z + lax.axis_index("z")
    m = lax.axis_index("xl") * Y + lax.axis_index("y")
    got = lax.all_to_all(sent, ("xh", "z", "xl", "y"), 0, 0, axis_index_groups=groups)
    return jnp.where(f > m, got[0], jnp.where(f < m, got[1], x))


def mirror_chips(x):
    chips = XH * Z
    perm = [(f * chips + m, m * chips + f) for f in range(chips) for m in range(chips)]
    return lax.ppermute(x, ("xh", "z", "xl", "y"), perm)


def swap(x, axis):
    return lax.ppermute(x, axis, [(0, 1), (1, 0)])


def product(swapped, act_all, near, far, parts):
    _, _, width, rows = act_all.shape
    cols = near.shape[2]
    tile = width // 2

    def kernel(swapped_ref, act_ref, near_ref, far_ref, *out_refs):
        def go(blocks):
            for t in range(width // tile):
                at = slice(t * tile, (t + 1) * tile)
                total = None
                for pair in range(2):
                    act = jnp.concatenate([act_ref[y, pair, at] for y in range(Y)], axis=1)
                    grad = jnp.concatenate([blocks[pair][y] for y in range(Y)], axis=0)
                    part = jnp.dot(act, grad, preferred_element_type=jnp.float32)
                    total = part if total is None else total + part
                if parts == 1:
                    out_refs[0][at] = total
                else:
                    out_refs[t][...] = total

        @pl.when(swapped_ref[0] == 0)
        def _():
            go((near_ref, far_ref))

        @pl.when(swapped_ref[0] != 0)
        def _():
            go((far_ref, near_ref))

    vmem = pl.BlockSpec(memory_space=pltpu.VMEM)
    return pl.pallas_call(
        kernel,
        in_specs=[pl.BlockSpec(memory_space=pltpu.SMEM), vmem, vmem, vmem],
        out_specs=[vmem] * parts,
        out_shape=[jax.ShapeDtypeStruct((width // parts, cols), jnp.float32)] * parts,
        compiler_params=pltpu.CompilerParams(vmem_limit_bytes=16 * 1024 * 1024),
        cost_estimate=pl.CostEstimate(
            flops=2 * width * cols * rows * 2 * Y,
            bytes_accessed=act_all.size * 2 + near.size * 4 + width * cols * 4,
            transcendentals=0,
        ),
    )(swapped, act_all, near, far)


def per_device(activations, act_basis, gradients, grad_basis):
    rows, act_width = activations.shape
    xh, xl, c = (lax.axis_index(a) for a in ("xh", "xl", "c"))

    grad_rot = jnp.dot(gradients, grad_basis, preferred_element_type=jnp.float32)
    grad_sq = (grad_rot * grad_rot).astype(jnp.bfloat16)
    cols = grad_sq.shape[1] // 2

    def half_of(half):
        return lax.dynamic_slice_in_dim(grad_sq, half * cols, cols, 1)

    grad_other, grad_mine = half_of(1 - c), half_of(c)
    grad_pair = jnp.broadcast_to(grad_other, (2,) + grad_other.shape)

    def rotated(act):
        blocks = act.reshape(rows, act_width // BLOCK, BLOCK)
        rot = jnp.einsum("tbk,bkj->bjt", blocks, act_basis, preferred_element_type=jnp.float32)
        return (rot * rot).astype(jnp.bfloat16).reshape(act_width, rows)

    others, _ = lax.optimization_barrier((swap(activations, "xl"), (grad_pair, grad_mine)))
    act_pair = jnp.stack([rotated(activations), rotated(others)])
    act_all = lax.all_gather(act_pair, "y", axis=0)

    def gathered(own):
        return lax.all_to_all(jnp.broadcast_to(own, (Z,) + own.shape), "z", 0, 0)

    near_other = gathered(transpose_chips(grad_other, grad_pair))
    near_mine = gathered(mirror_chips(grad_mine))
    far_other = swap(near_other, "xh")
    far_mine = swap(near_mine, "xh")
    swapped = (xh ^ xl)[None]
    act_all, _ = lax.optimization_barrier((act_all, near_mine))
    other = product(swapped, act_all, near_other, far_other, 2)
    got = [swap(part, "c") for part in other]
    (mine,) = product(swapped, act_all, near_mine, far_mine, 1)
    return (mine + jnp.concatenate(got)) / TOKENS


def solution(mesh):
    chips = Mesh(mesh.devices.reshape(XH, Z, XL, Y, C), ("xh", "z", "xl", "y", "c"))
    feat, tok = ("xh", "z"), ("xl", "y", "c")
    return jax.shard_map(
        per_device,
        mesh=chips,
        in_specs=(P(tok, feat), P(feat, None, None), P(tok, feat), P(feat, None)),
        out_specs=P(feat, tok),
        check_vma=False,
    )
```

```python
import jax
import jax.numpy as jnp
from jax import lax
from jax.experimental import pallas as pl
from jax.experimental.pallas import tpu as pltpu
from jax.sharding import Mesh
from jax.sharding import PartitionSpec as P

BLOCK = 512
TOKENS = 4096
XH, Z, XL, Y, C = 2, 8, 2, 8, 2


def transpose_chips(x, sent):
    chips = XH * Z
    swaps = [[f * chips + m, m * chips + f] for f in range(chips) for m in range(f + 1, chips)]
    fixed = [f * chips + f for f in range(chips)]
    groups = swaps + [[fixed[i], fixed[i + 1]] for i in range(0, chips, 2)]
    f = lax.axis_index("xh") * Z + lax.axis_index("z")
    m = lax.axis_index("xl") * Y + lax.axis_index("y")
    got = lax.all_to_all(sent, ("xh", "z", "xl", "y"), 0, 0, axis_index_groups=groups)
    return jnp.where(f > m, got[0], jnp.where(f < m, got[1], x))


def swap(x, axis):
    return lax.ppermute(x, axis, [(0, 1), (1, 0)])


def product(swapped, act_all, near, far, parts):
    _, _, width, rows = act_all.shape
    cols = near.shape[2]
    tile = width // 2

    def kernel(swapped_ref, act_ref, near_ref, far_ref, *out_refs):
        def go(blocks):
            for t in range(width // tile):
                at = slice(t * tile, (t + 1) * tile)
                total = None
                for pair in range(2):
                    act = jnp.concatenate([act_ref[y, pair, at] for y in range(Y)], axis=1)
                    grad = jnp.concatenate([blocks[pair][y] for y in range(Y)], axis=0)
                    part = jnp.dot(act, grad, preferred_element_type=jnp.float32)
                    total = part if total is None else total + part
                if parts == 1:
                    out_refs[0][at] = total
                else:
                    out_refs[t][...] = total

        @pl.when(swapped_ref[0] == 0)
        def _():
            go((near_ref, far_ref))

        @pl.when(swapped_ref[0] != 0)
        def _():
            go((far_ref, near_ref))

    vmem = pl.BlockSpec(memory_space=pltpu.VMEM)
    return pl.pallas_call(
        kernel,
        in_specs=[pl.BlockSpec(memory_space=pltpu.SMEM), vmem, vmem, vmem],
        out_specs=[vmem] * parts,
        out_shape=[jax.ShapeDtypeStruct((width // parts, cols), jnp.float32)] * parts,
        compiler_params=pltpu.CompilerParams(vmem_limit_bytes=16 * 1024 * 1024),
        cost_estimate=pl.CostEstimate(
            flops=2 * width * cols * rows * 2 * Y,
            bytes_accessed=act_all.size * 2 + near.size * 4 + width * cols * 4,
            transcendentals=0,
        ),
    )(swapped, act_all, near, far)


def copies(x, count):
    def kernel(x_ref, out_ref):
        out_ref[...] = jnp.broadcast_to(x_ref[...][None], out_ref.shape)

    vmem = pl.BlockSpec(memory_space=pltpu.VMEM)
    return pl.pallas_call(
        kernel,
        in_specs=[vmem],
        out_specs=vmem,
        out_shape=jax.ShapeDtypeStruct((count,) + x.shape, x.dtype),
        compiler_params=pltpu.CompilerParams(vmem_limit_bytes=16 * 1024 * 1024),
        cost_estimate=pl.CostEstimate(flops=50_000_000_000, bytes_accessed=(count + 1) * x.size * 2, transcendentals=0),
    )(x)


def per_device(activations, act_basis, gradients, grad_basis):
    rows, act_width = activations.shape
    xh, xl, c = (lax.axis_index(a) for a in ("xh", "xl", "c"))

    grad_rot = jnp.dot(gradients, grad_basis, preferred_element_type=jnp.float32)
    grad_sq = (grad_rot * grad_rot).astype(jnp.bfloat16)
    grad_pair = jnp.broadcast_to(grad_sq, (2,) + grad_sq.shape)
    own = transpose_chips(grad_sq, grad_pair)

    act_in = jnp.stack([activations, swap(activations, "xl")])
    act_in = act_in.reshape(2, rows, act_width // BLOCK, BLOCK)
    act_rot = jnp.einsum("ptbk,bkj->pbjt", act_in, act_basis, preferred_element_type=jnp.float32)
    act_pair = (act_rot * act_rot).astype(jnp.bfloat16).reshape(2, act_width, rows)
    act_all = lax.all_gather(act_pair, "y", axis=0)

    cols = own.shape[1] // 2

    def gathered(half):
        mine = lax.dynamic_slice_in_dim(own, half * cols, cols, 1)
        return lax.all_to_all(copies(mine, Z), "z", 0, 0)

    near_other, near_mine = gathered(1 - c), gathered(c)
    far_other = swap(near_other, "xh")
    far_mine = swap(near_mine, "xh")
    swapped = (xh ^ xl)[None]
    act_all, _ = lax.optimization_barrier((act_all, near_mine))
    other = product(swapped, act_all, near_other, far_other, 2)
    got = [swap(part, "c") for part in other]
    (mine,) = product(swapped, act_all, near_mine, far_mine, 1)
    return (mine + jnp.concatenate(got)) / TOKENS


def solution(mesh):
    chips = Mesh(mesh.devices.reshape(XH, Z, XL, Y, C), ("xh", "z", "xl", "y", "c"))
    feat, tok = ("xh", "z"), ("xl", "y", "c")
    return jax.shard_map(
        per_device,
        mesh=chips,
        in_specs=(P(tok, feat), P(feat, None, None), P(tok, feat), P(feat, None)),
        out_specs=P(feat, tok),
        check_vma=False,
    )
```

```python
import jax
import jax.numpy as jnp
from jax import lax
from jax.experimental import pallas as pl
from jax.experimental.pallas import tpu as pltpu
from jax.sharding import Mesh
from jax.sharding import PartitionSpec as P

BLOCK = 512
TOKENS = 4096
XH, Z, XL, Y, C = 2, 8, 2, 8, 2


def vmem():
    return pl.BlockSpec(memory_space=pltpu.VMEM)


def squared_pair(gradients, basis):
    def kernel(grad_ref, basis_ref, out_ref):
        rot = jnp.dot(grad_ref[...], basis_ref[...], preferred_element_type=jnp.float32)
        square = (rot * rot).astype(jnp.bfloat16)
        out_ref[0] = square
        out_ref[1] = square

    rows, width = gradients.shape
    return pl.pallas_call(
        kernel,
        in_specs=[vmem()] * 2,
        out_specs=vmem(),
        out_shape=jax.ShapeDtypeStruct((2, rows, width), jnp.bfloat16),
        compiler_params=pltpu.CompilerParams(vmem_limit_bytes=16 * 1024 * 1024),
        cost_estimate=pl.CostEstimate(
            flops=2 * rows * width * width, bytes_accessed=2 * (width + 3 * rows) * width, transcendentals=0
        ),
    )(gradients, basis)


def transposed_copies(pair, c):
    chips = XH * Z
    swaps = [[f * chips + m, m * chips + f] for f in range(chips) for m in range(f + 1, chips)]
    fixed = [f * chips + f for f in range(chips)]
    groups = swaps + [[fixed[i], fixed[i + 1]] for i in range(0, chips, 2)]
    f = lax.axis_index("xh") * Z + lax.axis_index("z")
    m = lax.axis_index("xl") * Y + lax.axis_index("y")
    got = lax.all_to_all(pair, ("xh", "z", "xl", "y"), 0, 0, axis_index_groups=groups)
    rows, cols = pair.shape[1], pair.shape[2] // 2

    def kernel(where_ref, pair_ref, got_ref, other_ref, mine_ref):
        def copy_from(ref, block):
            for out_ref, half in ((other_ref, 1 - where_ref[1]), (mine_ref, where_ref[1])):
                part = ref[block, :, pl.ds(pl.multiple_of(half * cols, cols), cols)]
                out_ref[...] = jnp.broadcast_to(part[None], out_ref.shape)

        @pl.when(where_ref[0] == 0)
        def _():
            copy_from(pair_ref, 0)

        @pl.when(where_ref[0] > 0)
        def _():
            copy_from(got_ref, 0)

        @pl.when(where_ref[0] < 0)
        def _():
            copy_from(got_ref, 1)

    return pl.pallas_call(
        kernel,
        in_specs=[pl.BlockSpec(memory_space=pltpu.SMEM), vmem(), vmem()],
        out_specs=[vmem()] * 2,
        out_shape=[jax.ShapeDtypeStruct((Z, rows, cols), pair.dtype)] * 2,
        compiler_params=pltpu.CompilerParams(vmem_limit_bytes=16 * 1024 * 1024),
        cost_estimate=pl.CostEstimate(flops=0, bytes_accessed=4 * (Z + 2) * rows * cols, transcendentals=0),
    )(jnp.stack([f - m, c]).astype(jnp.int32), pair, got)


def swap(x, axis):
    return lax.ppermute(x, axis, [(0, 1), (1, 0)])


def product(swapped, act_all, near, far, parts):
    _, _, width, rows = act_all.shape
    cols = near.shape[2]
    tile = width // 2

    def kernel(swapped_ref, act_ref, near_ref, far_ref, *out_refs):
        def go(blocks):
            for t in range(width // tile):
                at = slice(t * tile, (t + 1) * tile)
                total = None
                for pair in range(2):
                    act = jnp.concatenate([act_ref[y, pair, at] for y in range(Y)], axis=1)
                    grad = jnp.concatenate([blocks[pair][y] for y in range(Y)], axis=0)
                    part = jnp.dot(act, grad, preferred_element_type=jnp.float32)
                    total = part if total is None else total + part
                if parts == 1:
                    out_refs[0][at] = total
                else:
                    out_refs[t][...] = total

        @pl.when(swapped_ref[0] == 0)
        def _():
            go((near_ref, far_ref))

        @pl.when(swapped_ref[0] != 0)
        def _():
            go((far_ref, near_ref))

    vmem = pl.BlockSpec(memory_space=pltpu.VMEM)
    return pl.pallas_call(
        kernel,
        in_specs=[pl.BlockSpec(memory_space=pltpu.SMEM), vmem, vmem, vmem],
        out_specs=[vmem] * parts,
        out_shape=[jax.ShapeDtypeStruct((width // parts, cols), jnp.float32)] * parts,
        compiler_params=pltpu.CompilerParams(vmem_limit_bytes=16 * 1024 * 1024),
        cost_estimate=pl.CostEstimate(
            flops=2 * width * cols * rows * 2 * Y,
            bytes_accessed=act_all.size * 2 + near.size * 4 + width * cols * 4,
            transcendentals=0,
        ),
    )(swapped, act_all, near, far)


def per_device(activations, act_basis, gradients, grad_basis):
    rows, act_width = activations.shape
    xh, xl, c = (lax.axis_index(a) for a in ("xh", "xl", "c"))

    grad_pair = squared_pair(gradients, grad_basis)

    def rotated(act):
        blocks = act.reshape(rows, act_width // BLOCK, BLOCK)
        rot = jnp.einsum("tbk,bkj->bjt", blocks, act_basis, preferred_element_type=jnp.float32)
        return (rot * rot).astype(jnp.bfloat16).reshape(act_width, rows)

    others, _ = lax.optimization_barrier((swap(activations, "xl"), grad_pair))
    act_pair = jnp.stack([rotated(activations), rotated(others)])
    act_all = lax.all_gather(act_pair, "y", axis=0)

    copies_other, copies_mine = transposed_copies(grad_pair, c)
    near_other = lax.all_to_all(copies_other, "z", 0, 0)
    near_mine = lax.all_to_all(copies_mine, "z", 0, 0)
    far_other = swap(near_other, "xh")
    far_mine = swap(near_mine, "xh")
    swapped = (xh ^ xl)[None]
    act_all, _ = lax.optimization_barrier((act_all, near_mine))
    other = product(swapped, act_all, near_other, far_other, 2)
    got = [swap(part, "c") for part in other]
    (mine,) = product(swapped, act_all, near_mine, far_mine, 1)
    return (mine + jnp.concatenate(got)) / TOKENS


def solution(mesh):
    chips = Mesh(mesh.devices.reshape(XH, Z, XL, Y, C), ("xh", "z", "xl", "y", "c"))
    feat, tok = ("xh", "z"), ("xl", "y", "c")
    return jax.shard_map(
        per_device,
        mesh=chips,
        in_specs=(P(tok, feat), P(feat, None, None), P(tok, feat), P(feat, None)),
        out_specs=P(feat, tok),
        check_vma=False,
    )
```

```python
import jax
import jax.numpy as jnp
from jax import lax
from jax.experimental import pallas as pl
from jax.experimental.pallas import tpu as pltpu
from jax.sharding import Mesh
from jax.sharding import PartitionSpec as P

BLOCK = 512
TOKENS = 4096
XH, Z, XL, Y, C = 2, 8, 2, 8, 2


def vmem():
    return pl.BlockSpec(memory_space=pltpu.VMEM)


def squared_pair(gradients, basis):
    def kernel(grad_ref, basis_ref, out_ref):
        rot = jnp.dot(grad_ref[...], basis_ref[...], preferred_element_type=jnp.float32)
        square = (rot * rot).astype(jnp.bfloat16)
        out_ref[0] = square
        out_ref[1] = square

    rows, width = gradients.shape
    return pl.pallas_call(
        kernel,
        in_specs=[vmem()] * 2,
        out_specs=vmem(),
        out_shape=jax.ShapeDtypeStruct((2, rows, width), jnp.bfloat16),
        compiler_params=pltpu.CompilerParams(vmem_limit_bytes=16 * 1024 * 1024),
        cost_estimate=pl.CostEstimate(
            flops=2 * rows * width * width, bytes_accessed=2 * (width + 3 * rows) * width, transcendentals=0
        ),
    )(gradients, basis)


def transpose_chips(x, sent):
    chips = XH * Z
    swaps = [[f * chips + m, m * chips + f] for f in range(chips) for m in range(f + 1, chips)]
    fixed = [f * chips + f for f in range(chips)]
    groups = swaps + [[fixed[i], fixed[i + 1]] for i in range(0, chips, 2)]
    f = lax.axis_index("xh") * Z + lax.axis_index("z")
    m = lax.axis_index("xl") * Y + lax.axis_index("y")
    got = lax.all_to_all(sent, ("xh", "z", "xl", "y"), 0, 0, axis_index_groups=groups)
    return jnp.where(f > m, got[0], jnp.where(f < m, got[1], x))


def swap(x, axis):
    return lax.ppermute(x, axis, [(0, 1), (1, 0)])


def product(swapped, act_all, near, far, parts):
    _, _, width, rows = act_all.shape
    cols = near.shape[2]
    tile = width // 2

    def kernel(swapped_ref, act_ref, near_ref, far_ref, *out_refs):
        def go(blocks):
            for t in range(width // tile):
                at = slice(t * tile, (t + 1) * tile)
                total = None
                for pair in range(2):
                    act = jnp.concatenate([act_ref[y, pair, at] for y in range(Y)], axis=1)
                    grad = jnp.concatenate([blocks[pair][y] for y in range(Y)], axis=0)
                    part = jnp.dot(act, grad, preferred_element_type=jnp.float32)
                    total = part if total is None else total + part
                if parts == 1:
                    out_refs[0][at] = total
                else:
                    out_refs[t][...] = total

        @pl.when(swapped_ref[0] == 0)
        def _():
            go((near_ref, far_ref))

        @pl.when(swapped_ref[0] != 0)
        def _():
            go((far_ref, near_ref))

    vmem = pl.BlockSpec(memory_space=pltpu.VMEM)
    return pl.pallas_call(
        kernel,
        in_specs=[pl.BlockSpec(memory_space=pltpu.SMEM), vmem, vmem, vmem],
        out_specs=[vmem] * parts,
        out_shape=[jax.ShapeDtypeStruct((width // parts, cols), jnp.float32)] * parts,
        compiler_params=pltpu.CompilerParams(vmem_limit_bytes=16 * 1024 * 1024),
        cost_estimate=pl.CostEstimate(
            flops=2 * width * cols * rows * 2 * Y,
            bytes_accessed=act_all.size * 2 + near.size * 4 + width * cols * 4,
            transcendentals=0,
        ),
    )(swapped, act_all, near, far)


def per_device(activations, act_basis, gradients, grad_basis):
    rows, act_width = activations.shape
    xh, xl, c = (lax.axis_index(a) for a in ("xh", "xl", "c"))

    grad_pair = squared_pair(gradients, grad_basis)

    def rotated(act):
        blocks = act.reshape(rows, act_width // BLOCK, BLOCK)
        rot = jnp.einsum("tbk,bkj->bjt", blocks, act_basis, preferred_element_type=jnp.float32)
        return (rot * rot).astype(jnp.bfloat16).reshape(act_width, rows)

    others, _ = lax.optimization_barrier((swap(activations, "xl"), grad_pair))
    act_pair = jnp.stack([rotated(activations), rotated(others)])
    act_all = lax.all_gather(act_pair, "y", axis=0)

    own = transpose_chips(grad_pair[0], grad_pair)
    cols = own.shape[1] // 2

    def gathered(half):
        mine = lax.dynamic_slice_in_dim(own, half * cols, cols, 1)
        return lax.all_to_all(jnp.broadcast_to(mine, (Z,) + mine.shape), "z", 0, 0)

    near_other, near_mine = gathered(1 - c), gathered(c)
    far_other = swap(near_other, "xh")
    far_mine = swap(near_mine, "xh")
    swapped = (xh ^ xl)[None]
    act_all, _ = lax.optimization_barrier((act_all, near_mine))
    other = product(swapped, act_all, near_other, far_other, 2)
    got = [swap(part, "c") for part in other]
    (mine,) = product(swapped, act_all, near_mine, far_mine, 1)
    return (mine + jnp.concatenate(got)) / TOKENS


def solution(mesh):
    chips = Mesh(mesh.devices.reshape(XH, Z, XL, Y, C), ("xh", "z", "xl", "y", "c"))
    feat, tok = ("xh", "z"), ("xl", "y", "c")
    return jax.shard_map(
        per_device,
        mesh=chips,
        in_specs=(P(tok, feat), P(feat, None, None), P(tok, feat), P(feat, None)),
        out_specs=P(feat, tok),
        check_vma=False,
    )
```

```python
import jax
import jax.numpy as jnp
from jax import lax
from jax.experimental import pallas as pl
from jax.experimental.pallas import tpu as pltpu
from jax.sharding import Mesh
from jax.sharding import PartitionSpec as P

BLOCK = 512
TOKENS = 4096
XH, Z, XL, Y, C = 2, 8, 2, 8, 2


def transpose_chips(x, sent):
    chips = XH * Z
    swaps = [[f * chips + m, m * chips + f] for f in range(chips) for m in range(f + 1, chips)]
    fixed = [f * chips + f for f in range(chips)]
    groups = swaps + [[fixed[i], fixed[i + 1]] for i in range(0, chips, 2)]
    f = lax.axis_index("xh") * Z + lax.axis_index("z")
    m = lax.axis_index("xl") * Y + lax.axis_index("y")
    got = lax.all_to_all(sent, ("xh", "z", "xl", "y"), 0, 0, axis_index_groups=groups)
    return jnp.where(f > m, got[0], jnp.where(f < m, got[1], x))


def swap(x, axis):
    return lax.ppermute(x, axis, [(0, 1), (1, 0)])


def product(swapped, act_all, near, far, got=()):
    _, _, width, rows = act_all.shape
    cols = near.shape[2]
    tile = width // 2

    def kernel(swapped_ref, act_ref, near_ref, far_ref, *refs):
        got_refs, out_refs = refs[: len(got)], refs[len(got) :]

        def go(blocks):
            for t in range(width // tile):
                at = slice(t * tile, (t + 1) * tile)
                total = None
                for pair in range(2):
                    act = jnp.concatenate([act_ref[y, pair, at] for y in range(Y)], axis=1)
                    grad = jnp.concatenate([blocks[pair][y] for y in range(Y)], axis=0)
                    part = jnp.dot(act, grad, preferred_element_type=jnp.float32)
                    total = part if total is None else total + part
                if got:
                    out_refs[0][at] = (total + got_refs[t][...]) * (1.0 / TOKENS)
                else:
                    out_refs[t][...] = total

        @pl.when(swapped_ref[0] == 0)
        def _():
            go((near_ref, far_ref))

        @pl.when(swapped_ref[0] != 0)
        def _():
            go((far_ref, near_ref))

    vmem = pl.BlockSpec(memory_space=pltpu.VMEM)
    parts = 1 if got else 2
    return pl.pallas_call(
        kernel,
        in_specs=[pl.BlockSpec(memory_space=pltpu.SMEM)] + [vmem] * (3 + len(got)),
        out_specs=[vmem] * parts,
        out_shape=[jax.ShapeDtypeStruct((width // parts, cols), jnp.float32)] * parts,
        compiler_params=pltpu.CompilerParams(vmem_limit_bytes=16 * 1024 * 1024),
        cost_estimate=pl.CostEstimate(
            flops=2 * width * cols * rows * 2 * Y,
            bytes_accessed=act_all.size * 2 + near.size * 4 + width * cols * 4,
            transcendentals=0,
        ),
    )(swapped, act_all, near, far, *got)


def per_device(activations, act_basis, gradients, grad_basis):
    rows, act_width = activations.shape
    xh, xl, c = (lax.axis_index(a) for a in ("xh", "xl", "c"))

    grad_rot = jnp.dot(gradients, grad_basis, preferred_element_type=jnp.float32)
    grad_sq = (grad_rot * grad_rot).astype(jnp.bfloat16)
    grad_pair = jnp.broadcast_to(grad_sq, (2,) + grad_sq.shape)
    own = transpose_chips(grad_sq, grad_pair)

    def rotated(act):
        blocks = act.reshape(rows, act_width // BLOCK, BLOCK)
        rot = jnp.einsum("tbk,bkj->bjt", blocks, act_basis, preferred_element_type=jnp.float32)
        return (rot * rot).astype(jnp.bfloat16).reshape(act_width, rows)

    others, _ = lax.optimization_barrier((swap(activations, "xl"), grad_pair))
    act_pair = jnp.stack([rotated(activations), rotated(others)])
    act_all = lax.all_gather(act_pair, "y", axis=0)

    cols = own.shape[1] // 2

    def gathered(half):
        mine = lax.dynamic_slice_in_dim(own, half * cols, cols, 1)
        return lax.all_to_all(jnp.broadcast_to(mine, (Z,) + mine.shape), "z", 0, 0)

    near_other, near_mine = gathered(1 - c), gathered(c)
    far_other = swap(near_other, "xh")
    far_mine = swap(near_mine, "xh")
    swapped = (xh ^ xl)[None]
    act_all, _ = lax.optimization_barrier((act_all, near_mine))
    other = product(swapped, act_all, near_other, far_other)
    got = [swap(part, "c") for part in other]
    (moments,) = product(swapped, act_all, near_mine, far_mine, got)
    return moments


def solution(mesh):
    chips = Mesh(mesh.devices.reshape(XH, Z, XL, Y, C), ("xh", "z", "xl", "y", "c"))
    feat, tok = ("xh", "z"), ("xl", "y", "c")
    return jax.shard_map(
        per_device,
        mesh=chips,
        in_specs=(P(tok, feat), P(feat, None, None), P(tok, feat), P(feat, None)),
        out_specs=P(feat, tok),
        check_vma=False,
    )
```
